256 devices in a mesh: gz: 64 (over z_lo, x, y, core), gy: 4 (over z_hi).
Axes of the slice: x: 4, y: 4, z: 8 (z_hi: 4, z_lo: 2; z = z_hi * 2 + z_lo), core: 2. Of those that a mesh axis runs over, the one named last changes fastest.
Arguments:
- image0: float32 [256, 256, 256], P('gz', 'gy'), may hold values from 0 to 8
- image1: float32 [256, 256, 256], P('gz', 'gy'), may hold values from 0 to 8
- flow: float32 [3, 256, 256, 256], P(None, 'gz', 'gy'), may hold values from -6 to 6
- cotangent: float32 [3, 256, 256, 256], P(None, 'gz', 'gy'), may hold values from -4.5 to 4.5
Outputs:
- adjoint: float32 [3, 256, 256, 256], P(None, 'gz', 'gy')
- grad_image0: float32 [256, 256, 256], P('gz', 'gy')
- grad_image1: float32 [256, 256, 256], P('gz', 'gy')
The draws below stay inside these ranges and needn't reach their ends.
All inputs are finite; a program needn't handle non-finite values.
Results may differ from the reference program's by a relative error of at most 0.03.
Values sent between devices are 32-bit elements; how exact they have to be, the bound alone decides.
No kernel may reach another device: no remote copies, remote signals or barrier semaphores. Data moves between devices by JAX's collectives and lax.ppermute only.
A program may use at most 64 MiB of HBM per device.

```python
import math
import jax
import jax.numpy as jnp

NZ = 256
ITERS = 3
NX = 256
NY = 256


def coordinates():
    first = jnp.arange(NX, dtype=jnp.float32) / NX
    second = jnp.arange(NY, dtype=jnp.float32) / NY
    third = jnp.arange(NZ, dtype=jnp.float32) / NZ
    return (first, second, third)


def plane_wave(key, low, high):
    key_freq, key_phase, key_sign = jax.random.split(key, 3)
    freqs = jax.random.uniform(key_freq, (3,), jnp.float32, low, high)
    signs = jnp.where(jax.random.bernoulli(key_sign, 0.5, (3,)), 1.0, -1.0).astype(jnp.float32)
    phase = jax.random.uniform(key_phase, (), jnp.float32, 0.0, 2.0 * math.pi)
    first, second, third = coordinates()
    angle = freqs[0] * signs[0] * first[:, None, None]
    angle = angle + freqs[1] * signs[1] * second[None, :, None]
    angle = angle + freqs[2] * signs[2] * third[None, None, :]
    return jnp.sin(2.0 * math.pi * angle + phase)


def region(key, low, high):
    key_freq, key_phase = jax.random.split(key, 2)
    freqs = jax.random.uniform(key_freq, (2,), jnp.float32, low, high)
    phase = jax.random.uniform(key_phase, (), jnp.float32, 0.0, 2.0 * math.pi)
    first, second, third = coordinates()
    angle = freqs[0] * first[:, None, None] + 0.5 * freqs[1] * second[None, :, None]
    return 0.5 + 0.5 * jnp.sin(2.0 * math.pi * angle + phase)


def intensity_common(key, power, level):
    key_region, key_wave, key_noise = jax.random.split(key, 3)
    contrast = 0.4 + 2.0 * region(key_region, 1.0, 2.0)
    smooth = level * plane_wave(key_wave, 0.5, 2.0)
    raw = jax.random.uniform(key_noise, (NX, NY, NZ), jnp.float32, -1.0, 1.0)
    shared = jnp.sign(raw) * jnp.abs(raw) ** power
    return (contrast, smooth, shared)


def draw_image0(key, part):
    contrast, smooth, shared = intensity_common(key, 1.0, 0.8)
    key = jax.random.fold_in(key, 21)
    own = jax.random.uniform(key, (NX, NY, NZ), jnp.float32, -1.0, 1.0)
    return 4.0 + smooth + contrast * (0.7 * shared + 0.5 * own)


def draw_image1(key, part):
    contrast, smooth, shared = intensity_common(key, 1.0, 0.8)
    key = jax.random.fold_in(key, 22)
    own = jax.random.uniform(key, (NX, NY, NZ), jnp.float32, -1.0, 1.0)
    return 4.0 + smooth + contrast * (0.7 * shared + 0.5 * own)


def draw_cotangent(key, part):
    key = jax.random.fold_in(key, 31)
    key_region, key_wave, key_noise = jax.random.split(key, 3)
    rough = 0.1 + 0.9 * region(key_region, 1.0, 2.0)
    wave_keys = jax.random.split(key_wave, 9)
    components = []
    for comp in range(3):
        total = plane_wave(wave_keys[3 * comp], 0.5, 2.0)
        total = total + plane_wave(wave_keys[3 * comp + 1], 0.5, 2.0)
        total = total + plane_wave(wave_keys[3 * comp + 2], 0.5, 2.0)
        components.append(total)
    waves = jnp.stack(components)
    noise = jnp.clip(jax.random.normal(key_noise, (3, NX, NY, NZ), jnp.float32), -4.0, 4.0)
    smooth = 0.6 * waves
    return rough * noise + (1.1 - rough) * smooth


def shard_levels(rng, extent, shards, least, largest):
    def one(position, blocks):
        heights = jax.random.uniform(jax.random.fold_in(jax.random.fold_in(rng, 6), position), (blocks,), jnp.float32, least / len(shards), largest / len(shards))
        return jnp.repeat(jnp.exp(heights), extent[position] // blocks).reshape((-1,) + (1,) * (len(extent) - position - 1))

    gain = one(*shards[0])
    for cut in shards[1:]:
        gain = gain * one(*cut)
    return gain


def centred(rng, shape, scale, bound, cuts=(), held_as=jnp.bfloat16):
    level = shard_levels(rng, shape, cuts, -0.22, 0.18) if cuts else 1.0
    values = jax.random.normal(rng, shape, jnp.float32) * scale * level
    return jnp.minimum(jnp.maximum(values, -bound), bound).astype(held_as)


def setup_inputs(seed: int = 0) -> dict:
    seeds = jax.random.split(jax.random.key(seed), 5)
    image0 = draw_image0(jax.random.fold_in(seeds[4], 71), 0)
    image1 = draw_image1(jax.random.fold_in(seeds[4], 71), 0)
    flow = centred(seeds[2], (3, NX, NY, NZ), 1.0, 6.0, ((1, 64), (2, 4)), jnp.float32)
    cotangent = draw_cotangent(jax.random.fold_in(seeds[4], 71), 0)
    return dict(image0=image0, image1=image1, flow=flow, cotangent=cotangent)


smooth_weight = 0.5


def differences(field):
    padded = jnp.pad(field, 1)
    first = (padded[2:, 1:-1, 1:-1] - padded[:-2, 1:-1, 1:-1]) * 0.5
    second = (padded[1:-1, 2:, 1:-1] - padded[1:-1, :-2, 1:-1]) * 0.5
    third = (padded[1:-1, 1:-1, 2:] - padded[1:-1, 1:-1, :-2]) * 0.5
    return first, second, third


def laplace(field):
    padded = jnp.pad(field, ((0, 0), (1, 1), (1, 1), (1, 1)))
    beside = padded[:, 2:, 1:-1, 1:-1] + padded[:, :-2, 1:-1, 1:-1]
    beside = beside + padded[:, 1:-1, 2:, 1:-1] + padded[:, 1:-1, :-2, 1:-1]
    beside = beside + padded[:, 1:-1, 1:-1, 2:] + padded[:, 1:-1, 1:-1, :-2]
    return 6.0 * field - beside


def operate(field, gradient):
    return gradient * jnp.sum(gradient * field, axis=0) + smooth_weight * laplace(field)


def reference(image0, image1, flow, cotangent):
    average = (image0 + image1) * 0.5
    temporal = image1 - image0
    gradient = jnp.stack(differences(average))
    adjoint = jnp.zeros_like(cotangent)
    residual = cotangent
    direction = cotangent
    norm_now = jnp.sum(residual * residual)
    for iteration in range(ITERS):
        image = operate(direction, gradient)
        step_size = norm_now / jnp.sum(direction * image)
        adjoint = adjoint + step_size * direction
        residual = residual - step_size * image
        norm_next = jnp.sum(residual * residual)
        direction = residual + (norm_next / norm_now) * direction
        norm_now = norm_next
    along_adjoint = jnp.sum(gradient * adjoint, axis=0)
    along_flow = jnp.sum(gradient * flow, axis=0)
    coupling = -adjoint * (along_flow + temporal) - flow * along_adjoint
    spread = differences(coupling[0])[0] + differences(coupling[1])[1] + differences(coupling[2])[2]
    grad_image0 = -0.5 * spread + along_adjoint
    grad_image1 = -0.5 * spread - along_adjoint
    return adjoint, grad_image0, grad_image1
```

```python
import functools

import jax
import jax.numpy as jnp
from jax import lax
from jax.experimental import pallas as pl
from jax.experimental.pallas import tpu as pltpu
from jax.sharding import PartitionSpec as P

Z, Y, X = 4, 64, 256
R = Y + 8
PAD = R + 16
F32 = jnp.float32
VM = pl.BlockSpec(memory_space=pltpu.VMEM)
SM = pl.BlockSpec(memory_space=pltpu.SMEM)
PARAMS = pltpu.CompilerParams(vmem_limit_bytes=40 * 1024 * 1024)


def lane_sides(v):
    lane = lax.broadcasted_iota(jnp.int32, v.shape, v.ndim - 1)
    left = jnp.where(lane == 0, 0.0, pltpu.roll(v, 1, v.ndim - 1))
    right = jnp.where(lane == X - 1, 0.0, pltpu.roll(v, X - 1, v.ndim - 1))
    return left, right


def pack_rows(i0b, i1b, i0t, i1t, cb, ct, fb, ft, down, up, late_down, late_up):
    for out, late, a, b, c, f in ((down, late_down, i0b, i1b, cb, fb), (up, late_up, i0t, i1t, ct, ft)):
        out[0] = (a[...] + b[...]) * 0.5
        late[0] = b[...] - a[...]
        for k in range(3):
            out[k + 1] = c[k]
            late[k + 1] = f[k]


def pack_slabs(core, i0, i1, c, f, below, above, own, inner, outer, late_inner, late_outer):
    sub = lax.broadcasted_iota(jnp.int32, (8, X), 0)
    for z in range(Z):
        own[0, z, 0:Y] = (i0[z] + i1[z]) * 0.5
        for k in range(3):
            own[k + 1, z, 0:Y] = c[k, z]
        for k in range(4):
            own[k, z, Y:R] = jnp.where(sub < 3, above[k, z], jnp.where(sub >= 5, below[k, z], 0.0))
    is_one = core[0]
    for k in range(4):
        for z in range(3):
            inner[k, z] = own[k, z + 1 - is_one]
            outer[k, z] = own[k, z + is_one]
    top = (Z - 1) * (1 - is_one)
    low = (Z - 1) * is_one
    for out, z in ((late_inner, top), (late_outer, low)):
        out[0] = i1[z] - i0[z]
        for k in range(3):
            out[k + 1] = f[k, z]


def krylov(place, own, inner, outer, basis, grad, sums, ext, v1, v2):
    gz, gy = place[0], place[1]
    core = lax.rem(gz, 2)
    nz, ny = place[2], place[3]
    at_inner = 7 * (1 - core)
    at_outer = 7 * core

    def put(ref, k, z, value):
        ref[k, z, 8 : 8 + R] = value
        ref[k, z, 0:8] = value[R - 8 : R]
        ref[k, z, 8 + R : PAD] = value[0:8]

    for k in range(4):
        for z in range(Z):
            put(ext, k, z + 3, own[k, z])
        for z in range(3):
            put(ext, k, at_inner + z, inner[k, z])
            put(ext, k, at_outer + z, outer[k, z])

    row = lax.broadcasted_iota(jnp.int32, (24, X), 0) + (R - 24)
    keep = jnp.where(
        row < Y,
        1.0,
        jnp.where(row < Y + 4, jnp.where(gy < ny - 1, 1.0, 0.0), jnp.where(gy > 0, 1.0, 0.0)),
    )

    def inside(z):
        slab = gz * Z + z
        return jnp.where((slab >= 0) & (slab < nz * Z), 1.0, 0.0)

    def tiles(value, rows):
        total = value[0:8]
        for r in range(8, rows, 8):
            total = total + value[r : r + 8]
        return total

    def around(ref, k, z, r):
        v = ref[k, z, 8 + r : 32 + r]
        left, right = lane_sides(v)
        total = (ref[k, z, 9 + r : 33 + r] + ref[k, z, 7 + r : 31 + r]) + (left + right)
        return v, total + (ref[k, z + 1, 8 + r : 32 + r] + ref[k, z - 1, 8 + r : 32 + r])

    def store(ref, k, z, r, value):
        ref[k, z, 8 + r : 32 + r] = value
        if r == 0:
            ref[k, z, 8 + R : PAD] = value[0:8]
        if r == R - 24:
            ref[k, z, 0:8] = value[16:24]

    def apply(src, src_z, off, g, z, r):
        vs, around_all = [], []
        for k in range(3):
            v, total = around(src, k + off, src_z, r)
            vs.append(v)
            around_all.append(total)
        dot = g[0] * vs[0] + g[1] * vs[1] + g[2] * vs[2]
        return vs, [g[k] * dot + (3.0 * vs[k] - 0.5 * around_all[k]) for k in range(3)]

    zero = jnp.zeros((8, X), F32)

    def first(j, carry):
        m0, m1, m2 = carry
        e = j + 1
        z = j - 2
        scale = inside(z)
        mine = jnp.where((z >= 0) & (z < Z), 1.0, 0.0)
        t0, t1, t2 = zero, zero, zero
        for r in range(0, R, 24):
            rows = 24 if r < R - 24 else 16
            mid = ext[0, e, 8 + r : 32 + r]
            left, right = lane_sides(mid)
            g = [
                (ext[0, e + 1, 8 + r : 32 + r] - ext[0, e - 1, 8 + r : 32 + r]) * 0.5,
                (ext[0, e, 9 + r : 33 + r] - ext[0, e, 7 + r : 31 + r]) * 0.5,
                (right - left) * 0.5,
            ]
            for k in range(3):
                grad[k, j, r : r + 24] = g[k]
            vs, image = apply(ext, e, 1, g, z, r)
            for k in range(3):
                out = image[k] * scale
                if r == R - 24:
                    out = out * keep
                store(v1, k, j, r, out)
                t0 = t0 + tiles(vs[k] * vs[k], rows)
                t1 = t1 + tiles(vs[k] * out, rows)
                t2 = t2 + tiles(out * out, rows)
        return m0 + mine * t0, m1 + mine * t1, m2 + mine * t2

    m0, m1, m2 = lax.fori_loop(0, Z + 4, first, (zero, zero, zero))

    def second(j, carry):
        m3, m4 = carry
        z = j - 1
        scale = inside(z)
        mine = jnp.where((z >= 0) & (z < Z), 1.0, 0.0)
        t3, t4 = zero, zero
        for r in range(0, R, 24):
            rows = 24 if r < R - 24 else 16
            g = [grad[k, j + 1, r : r + 24] for k in range(3)]
            vs, image = apply(v1, j + 1, 0, g, z, r)
            for k in range(3):
                out = image[k] * scale
                if r == R - 24:
                    out = out * keep
                store(v2, k, j, r, out)
                basis[k, j, r : r + 24] = ext[k + 1, j + 2, 8 + r : 32 + r]
                basis[k + 3, j, r : r + 24] = vs[k]
                basis[k + 6, j, r : r + 24] = out
                t3 = t3 + tiles(vs[k] * out, rows)
                t4 = t4 + tiles(out * out, rows)
        return m3 + mine * t3, m4 + mine * t4

    m3, m4 = lax.fori_loop(0, Z + 2, second, (zero, zero))

    def third(z, m5):
        for r in range(0, R, 24):
            rows = 24 if r < R - 24 else 16
            g = [grad[k, z + 2, r : r + 24] for k in range(3)]
            vs, image = apply(v2, z + 1, 0, g, z, r)
            for k in range(3):
                m5 = m5 + tiles(vs[k] * image[k], rows)
        return m5

    m5 = lax.fori_loop(0, Z, third, zero)
    lane = lax.broadcasted_iota(jnp.int32, sums.shape, 1)
    out = jnp.zeros(sums.shape, F32)
    for k, m in enumerate((m0, m1, m2, m3, m4, m5)):
        out = jnp.where(lane == k, jnp.sum(m), out)
    sums[...] = out


def finish(core_ref, sums, basis, grad, i0, i1, f, late_below, late_above, late_inner, late_outer, adj, out0, out1, c0, c1, c2):
    total = jnp.sum(sums[...], axis=0, keepdims=True)
    m = [total[0, k] for k in range(6)]
    core = core_ref[0]
    a0 = m[0] / m[1]
    rr1 = m[0] - 2.0 * a0 * m[1] + a0 * a0 * m[2]
    b0 = rr1 / m[0]
    p10, p11 = 1.0 + b0, -a0
    a1 = rr1 / (p10 * p10 * m[1] + 2.0 * p10 * p11 * m[2] + p11 * p11 * m[3])
    r21, r22 = -a0 - a1 * p10, -a1 * p11
    rr2 = m[0] + r21 * r21 * m[2] + r22 * r22 * m[4] + 2.0 * (r21 * m[1] + r22 * m[2] + r21 * r22 * m[3])
    b1 = rr2 / rr1
    p20, p21, p22 = 1.0 + b1 * p10, r21 + b1 * p11, r22
    a2 = rr2 / (
        p20 * p20 * m[1] + p21 * p21 * m[3] + p22 * p22 * m[5]
        + 2.0 * (p20 * p21 * m[2] + p20 * p22 * m[3] + p21 * p22 * m[4])
    )
    w0 = a0 + a1 * p10 + a2 * p20
    w1 = a1 * p11 + a2 * p21
    w2 = a2 * p22

    def combine(z, lo, hi):
        a = [
            w0 * basis[k, z + 1, lo:hi] + w1 * basis[k + 3, z + 1, lo:hi] + w2 * basis[k + 6, z + 1, lo:hi]
            for k in range(3)
        ]
        g = [grad[k, z + 2, lo:hi] for k in range(3)]
        return a, g, g[0] * a[0] + g[1] * a[1] + g[2] * a[2]

    def edge(z, late):
        a, g, along = combine(z, 0, Y)
        rest = g[0] * late[1] + g[1] * late[2] + g[2] * late[3] + late[0]
        c0[z + 1] = -a[0] * rest - late[1] * along

    @pl.when(core == 0)
    def _():
        edge(-1, late_outer)
        edge(Z, late_inner)

    @pl.when(core == 1)
    def _():
        edge(-1, late_inner)
        edge(Z, late_outer)

    sub = lax.broadcasted_iota(jnp.int32, (8, X), 0)

    def slab(z, carry):
        a, g, along = combine(z, 0, Y)
        fl = [f[k, z] for k in range(3)]
        rest = g[0] * fl[0] + g[1] * fl[1] + g[2] * fl[2] + (i1[z] - i0[z])
        for k in range(3):
            adj[k, z] = a[k]
        c0[z + 1] = -a[0] * rest - fl[0] * along
        c1[z, 8 : 8 + Y] = -a[1] * rest - fl[1] * along
        c2[z] = -a[2] * rest - fl[2] * along
        out0[z] = along
        a, g, along = combine(z, Y, R)
        late = [jnp.where(sub < 4, late_above[k, z], late_below[k, z]) for k in range(4)]
        rest = g[0] * late[1] + g[1] * late[2] + g[2] * late[3] + late[0]
        side = -a[1] * rest - late[2] * along
        c1[z, 0:8] = side
        c1[z, 8 + Y : 16 + Y] = side
        return carry

    lax.fori_loop(0, Z, slab, 0)

    def spread(z, carry):
        left, right = lane_sides(c2[z])
        total = (c0[z + 2] - c0[z]) + (c1[z, 9 : 9 + Y] - c1[z, 7 : 7 + Y]) + (right - left)
        half = total * -0.25
        along = out0[z]
        out0[z] = half + along
        out1[z] = half - along
        return carry

    lax.fori_loop(0, Z, spread, 0)


def shape(*dims):
    return jax.ShapeDtypeStruct(dims, F32)


def shards(image0, image1, flow, cotangent):
    gz, gy = lax.axis_index("gz"), lax.axis_index("gy")
    nz, ny = lax.axis_size("gz"), lax.axis_size("gy")
    core = (gz % 2).astype(jnp.int32)[None]
    place = jnp.stack([gz, gy, jnp.int32(nz), jnp.int32(ny)]).astype(jnp.int32)

    bottom3 = pl.BlockSpec((Z, 8, X), lambda i: (0, 0, 0))
    top3 = pl.BlockSpec((Z, 8, X), lambda i: (0, Y // 8 - 1, 0))
    bottom4 = pl.BlockSpec((3, Z, 8, X), lambda i: (0, 0, 0, 0))
    top4 = pl.BlockSpec((3, Z, 8, X), lambda i: (0, 0, Y // 8 - 1, 0))
    down, up, late_down, late_up = pl.pallas_call(
        pack_rows,
        grid=(1,),
        in_specs=[bottom3, bottom3, top3, top3, bottom4, top4, bottom4, top4],
        out_specs=[VM] * 4,
        out_shape=[shape(4, Z, 8, X)] * 4,
        compiler_params=PARAMS,
        name="pack_rows",
    )(image0, image1, image0, image1, cotangent, cotangent, flow, flow)

    rise = [(i, i + 1) for i in range(ny - 1)]
    fall = [(i + 1, i) for i in range(ny - 1)]
    below = lax.ppermute(up, "gy", rise)
    above = lax.ppermute(down, "gy", fall)

    own, inner, outer, late_inner, late_outer = pl.pallas_call(
        pack_slabs,
        in_specs=[SM] + [VM] * 6,
        out_specs=[VM] * 5,
        out_shape=[shape(4, Z, R, X), shape(4, 3, R, X), shape(4, 3, R, X), shape(4, Y, X), shape(4, Y, X)],
        compiler_params=PARAMS,
        name="pack_slabs",
    )(core, image0, image1, cotangent, flow, below, above)

    mates = [(i, i ^ 1) for i in range(nz)]
    across = [(i, j) for i in range(nz) for j in [i - 1 if i % 2 == 0 else i + 1] if 0 <= j < nz]
    outer = lax.ppermute(outer, "gz", across)
    inner = lax.ppermute(inner, "gz", mates)
    late_outer = lax.ppermute(late_outer, "gz", across)
    late_inner = lax.ppermute(late_inner, "gz", mates)
    late_below = lax.ppermute(late_up, "gy", rise)
    late_above = lax.ppermute(late_down, "gy", fall)

    devices = nz * ny
    basis, grad, sums = pl.pallas_call(
        krylov,
        in_specs=[SM] + [VM] * 3,
        out_specs=[VM] * 3,
        out_shape=[shape(9, Z + 2, R, X), shape(3, Z + 4, R, X), shape(devices, 128)],
        scratch_shapes=[
            pltpu.VMEM((4, Z + 6, PAD, X), F32),
            pltpu.VMEM((3, Z + 4, PAD, X), F32),
            pltpu.VMEM((3, Z + 2, PAD, X), F32),
        ],
        compiler_params=PARAMS,
        name="krylov",
    )(place, own, inner, outer)

    sums = lax.all_to_all(sums.reshape(devices, 1, 128), ("gz", "gy"), 0, 0).reshape(devices, 128)

    return pl.pallas_call(
        finish,
        in_specs=[SM] + [VM] * 10,
        out_specs=[VM] * 3,
        out_shape=[shape(3, Z, Y, X), shape(Z, Y, X), shape(Z, Y, X)],
        scratch_shapes=[
            pltpu.VMEM((Z + 2, Y, X), F32),
            pltpu.VMEM((Z, Y + 16, X), F32),
            pltpu.VMEM((Z, Y, X), F32),
        ],
        compiler_params=PARAMS,
        name="finish",
    )(core, sums, basis, grad, image0, image1, flow, late_below, late_above, late_inner, late_outer)


def solution(mesh):
    return jax.shard_map(
        shards,
        mesh=mesh,
        in_specs=(
            P("gz", "gy", None),
            P("gz", "gy", None),
            P(None, "gz", "gy", None),
            P(None, "gz", "gy", None),
        ),
        out_specs=(P(None, "gz", "gy", None), P("gz", "gy", None), P("gz", "gy", None)),
        check_vma=False,
    )
```

```python
import functools

import jax
import jax.numpy as jnp
from jax import lax
from jax.experimental import pallas as pl
from jax.experimental.pallas import tpu as pltpu
from jax.sharding import PartitionSpec as P

Z, Y, X = 4, 64, 256
H = X // 2
R = Y + 8
PAD = R + 16
F32 = jnp.float32
VM = pl.BlockSpec(memory_space=pltpu.VMEM)
SM = pl.BlockSpec(memory_space=pltpu.SMEM)
HB = pl.BlockSpec(memory_space=pltpu.HBM)


def params(mib):
    return pltpu.CompilerParams(vmem_limit_bytes=mib * 1024 * 1024)


def lane_sides(v):
    lane = lax.broadcasted_iota(jnp.int32, v.shape[:-1] + (H,), v.ndim - 1)
    first, last = lane == 0, lane == H - 1
    a, b = v[..., :H], v[..., H:]
    ra, rb = pltpu.roll(a, 1, v.ndim - 1), pltpu.roll(b, 1, v.ndim - 1)
    qa, qb = pltpu.roll(a, H - 1, v.ndim - 1), pltpu.roll(b, H - 1, v.ndim - 1)
    left = jnp.concatenate([jnp.where(first, 0.0, ra), jnp.where(first, ra, rb)], axis=-1)
    right = jnp.concatenate([jnp.where(last, qb, qa), jnp.where(last, 0.0, qb)], axis=-1)
    return left, right


def pack_rows(place, i0, i1, c, f, side, middle, t0, t1, tc, tf, sems):
    copies = []
    for s, lo in enumerate((0, Y - 8)):
        rows = pl.ds(lo, 8)
        for n, (src, dst) in enumerate(((i0, t0), (i1, t1))):
            copies.append(pltpu.make_async_copy(src.at[:, rows], dst.at[s], sems.at[s, n]))
        for n, (src, dst) in enumerate(((c, tc), (f, tf))):
            copies.append(pltpu.make_async_copy(src.at[:, :, rows], dst.at[s], sems.at[s, n + 2]))
    for copy in copies:
        copy.start()
    for copy in copies:
        copy.wait()
    odd = lax.rem(place[1], 2) == 1
    sub = lax.broadcasted_iota(jnp.int32, (8, X), 0)

    def roll(v, n):
        return pltpu.roll(v, n, 0)

    for z in range(Z):
        messages = []
        for s in range(2):
            fields = [(t0[s, z] + t1[s, z]) * 0.5] + [tc[s, k, z] for k in range(3)]
            late = [t1[s, z] - t0[s, z]] + [tf[s, k, z] for k in range(3)]
            for p in range(2):
                one, two, one_late, two_late = fields[2 * p], fields[2 * p + 1], late[2 * p], late[2 * p + 1]
                if s == 0:
                    low, high, third, fourth = one, roll(two, 5), roll(one_late, 3), roll(two_late, 4)
                else:
                    low, high, third, fourth = roll(two, 3), one, roll(one_late, 4), roll(two_late, 5)
                messages.append(
                    jnp.where(sub < 3, low, jnp.where(sub == 3, third, jnp.where(sub == 4, fourth, high)))
                )
        for p in range(2):
            down, up = messages[p], messages[2 + p]
            side[p, z] = jnp.where(odd, down, up)
            middle[p, z] = jnp.where(odd, up, down)


def pack_slabs(place, i0, i1, c, f, side, middle, ring, late_rows, inner, outer, inner_far, outer_far):
    is_one = lax.rem(place[0], 2)
    odd = lax.rem(place[1], 2) == 1
    sub = lax.broadcasted_iota(jnp.int32, (8, X), 0)

    def roll(v, n):
        return pltpu.roll(v, n, 0)

    for z in range(Z):
        for p in range(2):
            a = jnp.where(odd, middle[p, z], side[p, z])
            b = jnp.where(odd, side[p, z], middle[p, z])
            ring[2 * p, z] = jnp.where(sub < 3, a, jnp.where(sub >= 5, b, 0.0))
            ring[2 * p + 1, z] = jnp.where(sub < 3, roll(a, 3), jnp.where(sub >= 5, roll(b, 5), 0.0))
            late_rows[2 * p, z] = jnp.where(sub == 0, roll(a, 5), roll(b, 4))
            late_rows[2 * p + 1, z] = jnp.where(sub == 0, roll(a, 4), roll(b, 3))
    for near, far, first, step in (
        (inner, inner_far, (Z - 1) * (1 - is_one), 2 * is_one - 1),
        (outer, outer_far, (Z - 1) * is_one, 1 - 2 * is_one),
    ):
        for d in range(3):
            z = first + d * step
            near[d, 0:Y] = (i0[z] + i1[z]) * 0.5
            near[d, Y:R] = ring[0, z]
            for k in range(3):
                if d < 2:
                    near[3 + 2 * k + d, 0:Y] = c[k, z]
                    near[3 + 2 * k + d, Y:R] = ring[k + 1, z]
                else:
                    far[k, 0:Y] = c[k, z]
                    far[k, Y:R] = ring[k + 1, z]
        far[3, 0:Y] = i1[first] - i0[first]
        for k in range(3):
            far[4 + k, 0:Y] = f[k, first]
        for k in range(4):
            far[3 + k, Y:R] = jnp.zeros((8, X), F32)


class Stencil:
    def __init__(self, place):
        self.gz, gy, self.nz, ny = (place[n] for n in range(4))
        row = lax.broadcasted_iota(jnp.int32, (24, X), 0) + (R - 24)
        after = jnp.where(gy < ny - 1, 1.0, 0.0)
        before = jnp.where(gy > 0, 1.0, 0.0)
        self.keep = jnp.where(row < Y, 1.0, jnp.where(row < Y + 4, after, before))

    def inside(self, z):
        slab = self.gz * Z + z
        return jnp.where((slab >= 0) & (slab < self.nz * Z), 1.0, 0.0)

    def mask(self, value, z, r):
        value = value * self.inside(z)
        return value * self.keep if r == R - 24 else value


def tiles(value, rows):
    total = value[0:8]
    for r in range(8, rows, 8):
        total = total + value[r : r + 8]
    return total


def put(ref, k, z, r, value):
    rows = value.shape[0]
    ref[k, z, 8 + r : 8 + r + rows] = value
    if r == 0:
        ref[k, z, 8 + R : PAD] = value[0:8]
    if r + rows == R:
        ref[k, z, 0:8] = value[rows - 8 : rows]


def row_sides(ref, k, z, r):
    return ref[k, z, 7 + r : 31 + r], ref[k, z, 9 + r : 33 + r]


def apply(g, vs, sums):
    dot = g[0] * vs[0] + g[1] * vs[1] + g[2] * vs[2]
    return [g[k] * dot + (3.0 * vs[k] - 0.5 * sums[k]) for k in range(3)]


def flat(ref, k, z, r):
    v = ref[k, z, 8 + r : 32 + r]
    left, right = lane_sides(v)
    before, after = row_sides(ref, k, z, r)
    return v, (before + after) + (left + right)


def krylov_near(place, i0, i1, c, ring, inner, outer, bs, v1, v2, grad, sums, mean, b):
    st = Stencil(place)
    is_one = lax.rem(st.gz, 2)
    for z in range(Z):
        put(mean, 0, z + 3, 0, (i0[z] + i1[z]) * 0.5)
        put(mean, 0, z + 3, Y, ring[0, z])
        for k in range(3):
            put(b, k, z + 2, 0, c[k, z])
            put(b, k, z + 2, Y, ring[k + 1, z])
            bs[k, z + 1, 0:Y] = c[k, z]
            bs[k, z + 1, Y:R] = ring[k + 1, z]
    for near, upper in ((inner, 1 - is_one), (outer, is_one)):
        for d in range(3):
            at = jnp.where(upper == 1, Z + d, -1 - d)
            put(mean, 0, at + 3, 0, near[d])
            for k in range(3):
                if d < 2:
                    put(b, k, at + 2, 0, near[3 + 2 * k + d])
                if d < 1:
                    bs[k, at + 1] = near[3 + 2 * k + d]

    zero = jnp.zeros((8, X), F32)

    def gradient(j, carry):
        for r in range(0, R, 24):
            left, right = lane_sides(mean[0, j + 1, 8 + r : 32 + r])
            before, after = row_sides(mean, 0, j + 1, r)
            grad[0, j, r : r + 24] = (mean[0, j + 2, 8 + r : 32 + r] - mean[0, j, 8 + r : 32 + r]) * 0.5
            grad[1, j, r : r + 24] = (after - before) * 0.5
            grad[2, j, r : r + 24] = (right - left) * 0.5
        return carry

    lax.fori_loop(0, Z + 4, gradient, 0)

    def first(j, carry):
        z = j - 1
        mine = jnp.where((z >= 0) & (z < Z), 1.0, 0.0)
        parts = [zero] * 3
        for r in range(0, R, 24):
            rows = 24 if r < R - 24 else 16
            g = [grad[k, j + 1, r : r + 24] for k in range(3)]
            vs, totals = [], []
            for k in range(3):
                v, total = flat(b, k, j + 1, r)
                vs.append(v)
                totals.append(total + (b[k, j, 8 + r : 32 + r] + b[k, j + 2, 8 + r : 32 + r]))
            for k, image in enumerate(apply(g, vs, totals)):
                out = st.mask(image, z, r)
                put(v1, k, j, r, out)
                for n, product in enumerate((vs[k] * vs[k], vs[k] * out, out * out)):
                    parts[n] = parts[n] + tiles(product, rows)
        return tuple(m + mine * t for m, t in zip(carry, parts))

    m0, m1, m2 = lax.fori_loop(0, Z + 2, first, (zero,) * 3)

    def second(z, carry):
        m3, m4 = carry
        for r in range(0, R, 24):
            rows = 24 if r < R - 24 else 16
            g = [grad[k, z + 2, r : r + 24] for k in range(3)]
            vs, totals = [], []
            for k in range(3):
                v, total = flat(v1, k, z + 1, r)
                vs.append(v)
                totals.append(total + (v1[k, z, 8 + r : 32 + r] + v1[k, z + 2, 8 + r : 32 + r]))
            for k, image in enumerate(apply(g, vs, totals)):
                out = st.mask(image, z, r)
                put(v2, k, z + 1, r, out)
                m3 = m3 + tiles(vs[k] * out, rows)
                m4 = m4 + tiles(out * out, rows)
        return m3, m4

    m3, m4 = lax.fori_loop(0, Z, second, (zero,) * 2)

    def third(z, m5):
        low = jnp.where(z > 0, 1.0, 0.0)
        for r in range(0, R, 24):
            rows = 24 if r < R - 24 else 16
            dot = 0.0
            for k in range(3):
                v, total = flat(v2, k, z + 1, r)
                dot = dot + grad[k, z + 2, r : r + 24] * v
                below = v2[k, jnp.maximum(z, 1), 8 + r : 32 + r] * low
                m5 = m5 + tiles(v * (3.0 * v - 0.5 * total - below), rows)
            m5 = m5 + tiles(dot * dot, rows)
        return m5

    m5 = lax.fori_loop(0, Z, third, zero)
    for n, m in enumerate((m0, m1, m2, m3, m4, m5)):
        sums[n] = m


def krylov_far(place, inner, outer, inner_far, outer_far, v1, v2, grad, near_sums, v2_far, late, sums, b, v1_far):
    st = Stencil(place)
    is_one = lax.rem(st.gz, 2)
    for near, far, side in ((inner, inner_far, 1 - is_one), (outer, outer_far, is_one)):
        for k in range(3):
            put(b, k, side, 0, near[4 + 2 * k])
            b[3 + k, side, 0:R] = near[3 + 2 * k]
            b[6 + k, side, 0:R] = far[k]
        for k in range(4):
            late[side, k] = far[3 + k, 0:Y]
    cross = jnp.zeros((8, X), F32)
    for side, z2, z1, edge in ((0, -2, -1, 0), (1, Z + 1, Z, Z - 1)):
        for r in range(0, R, 24):
            g = [grad[k, z2 + 2, r : r + 24] for k in range(3)]
            vs, totals = [], []
            for k in range(3):
                v, total = flat(b, k, side, r)
                vs.append(v)
                totals.append(total + (b[3 + k, side, r : r + 24] + b[6 + k, side, r : r + 24]))
            for k, image in enumerate(apply(g, vs, totals)):
                v1_far[k, side, r : r + 24] = st.mask(image, z2, r)
        for r in range(0, R, 24):
            rows = 24 if r < R - 24 else 16
            g = [grad[k, z1 + 2, r : r + 24] for k in range(3)]
            vs, totals = [], []
            for k in range(3):
                v, total = flat(v1, k, z1 + 1, r)
                vs.append(v)
                totals.append(total + (v1_far[k, side, r : r + 24] + v1[k, edge + 1, 8 + r : 32 + r]))
            for k, image in enumerate(apply(g, vs, totals)):
                out = st.mask(image, z1, r)
                v2_far[k, side, r : r + 24] = out
                cross = cross + tiles(v2[k, edge + 1, 8 + r : 32 + r] * out, rows)
    lane = lax.broadcasted_iota(jnp.int32, sums.shape, 1)
    out = jnp.zeros(sums.shape, F32)
    for n in range(6):
        m = near_sums[n] - 0.5 * cross if n == 5 else near_sums[n]
        out = jnp.where(lane == n, jnp.sum(m), out)
    sums[...] = out


def finish(sums, b, v1, v2, v2_far, grad, i0, i1, f, late_rows, late, adj, out0, out1, c0, c1, c2):
    total = jnp.sum(sums[...], axis=0, keepdims=True)
    m = [total[0, k] for k in range(6)]
    a0 = m[0] / m[1]
    rr1 = m[0] - 2.0 * a0 * m[1] + a0 * a0 * m[2]
    b0 = rr1 / m[0]
    p10, p11 = 1.0 + b0, -a0
    a1 = rr1 / (p10 * p10 * m[1] + 2.0 * p10 * p11 * m[2] + p11 * p11 * m[3])
    r21, r22 = -a0 - a1 * p10, -a1 * p11
    rr2 = m[0] + r21 * r21 * m[2] + r22 * r22 * m[4] + 2.0 * (r21 * m[1] + r22 * m[2] + r21 * r22 * m[3])
    b1 = rr2 / rr1
    p20, p21, p22 = 1.0 + b1 * p10, r21 + b1 * p11, r22
    a2 = rr2 / (
        p20 * p20 * m[1] + p21 * p21 * m[3] + p22 * p22 * m[5]
        + 2.0 * (p20 * p21 * m[2] + p20 * p22 * m[3] + p21 * p22 * m[4])
    )
    w0 = a0 + a1 * p10 + a2 * p20
    w1 = a1 * p11 + a2 * p21
    w2 = a2 * p22

    def combine(z, lo, hi, last):
        a = [
            w0 * b[k, z + 1, lo:hi] + w1 * v1[k, z + 1, 8 + lo : 8 + hi] + w2 * last(k)
            for k in range(3)
        ]
        g = [grad[k, z + 2, lo:hi] for k in range(3)]
        return a, g, g[0] * a[0] + g[1] * a[1] + g[2] * a[2]

    for side, z in ((0, -1), (1, Z)):
        a, g, along = combine(z, 0, Y, lambda k: v2_far[k, side, 0:Y])
        rest = g[0] * late[side, 1] + g[1] * late[side, 2] + g[2] * late[side, 3] + late[side, 0]
        c0[z + 1] = -a[0] * rest - late[side, 1] * along

    def slab(z, carry):
        a, g, along = combine(z, 0, Y, lambda k: v2[k, z + 1, 8 : 8 + Y])
        fl = [f[k, z] for k in range(3)]
        rest = g[0] * fl[0] + g[1] * fl[1] + g[2] * fl[2] + (i1[z] - i0[z])
        for k in range(3):
            adj[k, z] = a[k]
        c0[z + 1] = -a[0] * rest - fl[0] * along
        c1[z, 8 : 8 + Y] = -a[1] * rest - fl[1] * along
        c2[z] = -a[2] * rest - fl[2] * along
        out0[z] = along
        a, g, along = combine(z, Y, R, lambda k: v2[k, z + 1, 8 + Y : 8 + R])
        rows = [late_rows[k, z] for k in range(4)]
        rest = g[0] * rows[1] + g[1] * rows[2] + g[2] * rows[3] + rows[0]
        side = -a[1] * rest - rows[2] * along
        c1[z, 0:8] = side
        c1[z, 8 + Y : 16 + Y] = side
        return carry

    lax.fori_loop(0, Z, slab, 0)

    def spread(z, carry):
        left, right = lane_sides(c2[z])
        total = (c0[z + 2] - c0[z]) + (c1[z, 9 : 9 + Y] - c1[z, 7 : 7 + Y]) + (right - left)
        half = total * -0.25
        along = out0[z]
        out0[z] = half + along
        out1[z] = half - along
        return carry

    lax.fori_loop(0, Z, spread, 0)


def vmem(*dims):
    return pltpu.VMEM(dims, F32)


def pinned(array):
    return pltpu.with_memory_space_constraint(array, pltpu.VMEM)


def hbm(*arrays):
    return [pltpu.with_memory_space_constraint(array, pltpu.HBM) for array in arrays]


def shape(*dims):
    return jax.ShapeDtypeStruct(dims, F32)


def shards(image0, image1, flow, cotangent):
    gz, gy = lax.axis_index("gz"), lax.axis_index("gy")
    nz, ny = lax.axis_size("gz"), lax.axis_size("gy")
    place = jnp.stack([gz, gy, jnp.int32(nz), jnp.int32(ny)]).astype(jnp.int32)
    devices = nz * ny

    side, middle = pl.pallas_call(
        pack_rows,
        in_specs=[SM] + [HB] * 4,
        out_specs=[VM] * 2,
        out_shape=[vmem(2, Z, 8, X)] * 2,
        scratch_shapes=[
            pltpu.VMEM((2, Z, 8, X), F32),
            pltpu.VMEM((2, Z, 8, X), F32),
            pltpu.VMEM((2, 3, Z, 8, X), F32),
            pltpu.VMEM((2, 3, Z, 8, X), F32),
            pltpu.SemaphoreType.DMA((2, 4)),
        ],
        compiler_params=params(8),
        name="pack_rows",
    )(place, *hbm(image0, image1, cotangent, flow))

    def swaps(count, start):
        pairs = [(i, i + 1) for i in range(start, count - 1, 2)]
        return pairs + [(j, i) for i, j in pairs]

    middle = lax.ppermute(middle, "gy", swaps(ny, 1))
    side = lax.ppermute(side, "gy", swaps(ny, 0))

    ring, late_rows, inner, outer, inner_far, outer_far = pl.pallas_call(
        pack_slabs,
        in_specs=[SM] + [VM] * 6,
        out_specs=[VM] * 6,
        out_shape=[vmem(4, Z, 8, X)] * 2 + [vmem(9, R, X)] * 2 + [vmem(7, R, X)] * 2,
        compiler_params=params(8),
        name="pack_slabs",
    )(place, image0, image1, cotangent, flow, pinned(side), pinned(middle))
    outer = lax.ppermute(outer, "gz", swaps(nz, 1))
    inner = lax.ppermute(inner, "gz", swaps(nz, 0))
    outer_far = lax.ppermute(outer_far, "gz", swaps(nz, 1))
    inner_far = lax.ppermute(inner_far, "gz", swaps(nz, 0))
    inner, outer = pinned(inner), pinned(outer)

    b, v1, v2, grad, near_sums = pl.pallas_call(
        krylov_near,
        in_specs=[SM] + [VM] * 6,
        out_specs=[VM] * 5,
        out_shape=[
            vmem(3, Z + 2, R, X),
            vmem(3, Z + 2, PAD, X),
            vmem(3, Z + 2, PAD, X),
            vmem(3, Z + 4, R, X),
            vmem(6, 8, X),
        ],
        scratch_shapes=[pltpu.VMEM((1, Z + 6, PAD, X), F32), pltpu.VMEM((3, Z + 4, PAD, X), F32)],
        compiler_params=params(16),
        name="krylov_near",
    )(place, image0, image1, cotangent, ring, inner, outer)

    v2_far, late, sums = pl.pallas_call(
        krylov_far,
        in_specs=[SM] + [VM] * 8,
        out_specs=[VM] * 3,
        out_shape=[vmem(3, 2, R, X), vmem(2, 4, Y, X), vmem(devices, 128)],
        scratch_shapes=[pltpu.VMEM((9, 2, PAD, X), F32), pltpu.VMEM((3, 2, R, X), F32)],
        compiler_params=params(12),
        name="krylov_far",
    )(place, inner, outer, pinned(inner_far), pinned(outer_far), v1, v2, grad, near_sums)

    sums = lax.all_to_all(sums.reshape(devices, 1, 128), ("gz", "gy"), 0, 0).reshape(devices, 128)

    return pl.pallas_call(
        finish,
        in_specs=[VM] * 11,
        out_specs=[VM] * 3,
        out_shape=[shape(3, Z, Y, X), shape(Z, Y, X), shape(Z, Y, X)],
        scratch_shapes=[
            pltpu.VMEM((Z + 2, Y, X), F32),
            pltpu.VMEM((Z, Y + 16, X), F32),
            pltpu.VMEM((Z, Y, X), F32),
        ],
        compiler_params=params(12),
        name="finish",
    )(sums, b, v1, v2, v2_far, grad, image0, image1, flow, late_rows, late)


def solution(mesh):
    return jax.shard_map(
        shards,
        mesh=mesh,
        in_specs=(
            P("gz", "gy", None),
            P("gz", "gy", None),
            P(None, "gz", "gy", None),
            P(None, "gz", "gy", None),
        ),
        out_specs=(P(None, "gz", "gy", None), P("gz", "gy", None), P("gz", "gy", None)),
        check_vma=False,
    )
```

```python
import functools

import jax
import jax.numpy as jnp
from jax import lax
from jax.experimental import pallas as pl
from jax.experimental.pallas import tpu as pltpu
from jax.sharding import PartitionSpec as P

Z, Y, X = 4, 64, 256
H = X // 2
R = Y + 8
PAD = R + 16
F32 = jnp.float32
VM = pl.BlockSpec(memory_space=pltpu.VMEM)
SM = pl.BlockSpec(memory_space=pltpu.SMEM)
HB = pl.BlockSpec(memory_space=pltpu.HBM)


def params(mib):
    return pltpu.CompilerParams(vmem_limit_bytes=mib * 1024 * 1024)


def lane_sides(v):
    lane = lax.broadcasted_iota(jnp.int32, v.shape[:-1] + (H,), v.ndim - 1)
    first, last = lane == 0, lane == H - 1
    a, b = v[..., :H], v[..., H:]
    ra, rb = pltpu.roll(a, 1, v.ndim - 1), pltpu.roll(b, 1, v.ndim - 1)
    qa, qb = pltpu.roll(a, H - 1, v.ndim - 1), pltpu.roll(b, H - 1, v.ndim - 1)
    left = jnp.concatenate([jnp.where(first, 0.0, ra), jnp.where(first, ra, rb)], axis=-1)
    right = jnp.concatenate([jnp.where(last, qb, qa), jnp.where(last, 0.0, qb)], axis=-1)
    return left, right


def pack_rows(place, i0, i1, c, f, side, middle, t0, t1, tc, tf, sems):
    copies = []
    for s, lo in enumerate((0, Y - 8)):
        rows = pl.ds(lo, 8)
        for n, (src, dst) in enumerate(((i0, t0), (i1, t1))):
            copies.append(pltpu.make_async_copy(src.at[:, rows], dst.at[s], sems.at[s, n]))
        for n, (src, dst) in enumerate(((c, tc), (f, tf))):
            copies.append(pltpu.make_async_copy(src.at[:, :, rows], dst.at[s], sems.at[s, n + 2]))
    for copy in copies:
        copy.start()
    for copy in copies:
        copy.wait()
    odd = lax.rem(place[1], 2) == 1
    sub = lax.broadcasted_iota(jnp.int32, (8, X), 0)

    def roll(v, n):
        return pltpu.roll(v, n, 0)

    for z in range(Z):
        messages = []
        for s in range(2):
            fields = [(t0[s, z] + t1[s, z]) * 0.5] + [tc[s, k, z] for k in range(3)]
            late = [t1[s, z] - t0[s, z]] + [tf[s, k, z] for k in range(3)]
            for p in range(2):
                one, two, one_late, two_late = fields[2 * p], fields[2 * p + 1], late[2 * p], late[2 * p + 1]
                if s == 0:
                    low, high, third, fourth = one, roll(two, 5), roll(one_late, 3), roll(two_late, 4)
                else:
                    low, high, third, fourth = roll(two, 3), one, roll(one_late, 4), roll(two_late, 5)
                messages.append(
                    jnp.where(sub < 3, low, jnp.where(sub == 3, third, jnp.where(sub == 4, fourth, high)))
                )
        for p in range(2):
            down, up = messages[p], messages[2 + p]
            side[p, z] = jnp.where(odd, down, up)
            middle[p, z] = jnp.where(odd, up, down)


def pack_slabs(place, i0, i1, c, f, middle, side, ring, late_rows, inner, outer, inner_far, outer_far):
    is_one = lax.rem(place[0], 2)
    odd = lax.rem(place[1], 2) == 1
    sub = lax.broadcasted_iota(jnp.int32, (8, X), 0)

    def roll(v, n):
        return pltpu.roll(v, n, 0)

    for z in range(Z):
        for p in range(2):
            a = jnp.where(odd, middle[p, z], side[p, z])
            b = jnp.where(odd, side[p, z], middle[p, z])
            ring[2 * p, z] = jnp.where(sub < 3, a, jnp.where(sub >= 5, b, 0.0))
            ring[2 * p + 1, z] = jnp.where(sub < 3, roll(a, 3), jnp.where(sub >= 5, roll(b, 5), 0.0))
            late_rows[2 * p, z] = jnp.where(sub == 0, roll(a, 5), roll(b, 4))
            late_rows[2 * p + 1, z] = jnp.where(sub == 0, roll(a, 4), roll(b, 3))
    for near, far, first, step in (
        (inner, inner_far, (Z - 1) * (1 - is_one), 2 * is_one - 1),
        (outer, outer_far, (Z - 1) * is_one, 1 - 2 * is_one),
    ):
        for d in range(3):
            z = first + d * step
            for k in range(4):
                out, at = (near, 2 * k + d) if d < 2 else (far, k)
                out[at, 0:Y] = c[k - 1, z] if k else (i0[z] + i1[z]) * 0.5
                out[at, Y:R] = ring[k, z]
        mean = near[0]
        left, right = lane_sides(mean[0:Y])
        along_rows = pltpu.roll(mean, R - 1, 0)[0:Y] - pltpu.roll(mean, 1, 0)[0:Y]
        far[4, 0:Y] = (along_rows * f[1, first] + (right - left) * f[2, first]) * 0.5 + (i1[first] - i0[first])
        far[5, 0:Y] = f[0, first]
        for k in range(2):
            far[4 + k, Y:R] = jnp.zeros((8, X), F32)


class Stencil:
    def __init__(self, place):
        self.gz, gy, self.nz, ny = (place[n] for n in range(4))
        row = lax.broadcasted_iota(jnp.int32, (24, X), 0) + (R - 24)
        after = jnp.where(gy < ny - 1, 1.0, 0.0)
        before = jnp.where(gy > 0, 1.0, 0.0)
        self.keep = jnp.where(row < Y, 1.0, jnp.where(row < Y + 4, after, before))

    def inside(self, z):
        slab = self.gz * Z + z
        return jnp.where((slab >= 0) & (slab < self.nz * Z), 1.0, 0.0)

    def mask(self, value, z, r):
        value = value * self.inside(z)
        return value * self.keep if r == R - 24 else value


def tiles(value, rows):
    total = value[0:8]
    for r in range(8, rows, 8):
        total = total + value[r : r + 8]
    return total


def put(ref, k, z, r, value):
    rows = value.shape[0]
    ref[k, z, 8 + r : 8 + r + rows] = value
    if r == 0:
        ref[k, z, 8 + R : PAD] = value[0:8]
    if r + rows == R:
        ref[k, z, 0:8] = value[rows - 8 : rows]


def row_sides(ref, k, z, r):
    return ref[k, z, 7 + r : 31 + r], ref[k, z, 9 + r : 33 + r]


def apply(g, vs, sums):
    dot = g[0] * vs[0] + g[1] * vs[1] + g[2] * vs[2]
    return [g[k] * dot + (3.0 * vs[k] - 0.5 * sums[k]) for k in range(3)]


def flat(ref, k, z, r):
    v = ref[k, z, 8 + r : 32 + r]
    left, right = lane_sides(v)
    before, after = row_sides(ref, k, z, r)
    return v, (before + after) + (left + right)


def gradient(before, after, here, row_before, row_after):
    left, right = lane_sides(here)
    return [(after - before) * 0.5, (row_after - row_before) * 0.5, (right - left) * 0.5]


def first_step(st, mean, b, at, z, r, grad_to, put_to, parts):
    rows = 24 if r < R - 24 else 16
    mid = slice(8 + r, 32 + r)
    g = gradient(mean[0, at - 1, mid], mean[0, at + 1, mid], mean[0, at, mid], *row_sides(mean, 0, at, r))
    vs, totals = [], []
    for k in range(3):
        grad_to(k, g[k])
        v, total = flat(b, k, at, r)
        vs.append(v)
        totals.append(total + (b[k, at - 1, mid] + b[k, at + 1, mid]))
    parts = list(parts)
    for k, image in enumerate(apply(g, vs, totals)):
        out = st.mask(image, z, r)
        put_to(k, out)
        for n, product in enumerate((vs[k] * vs[k], vs[k] * out, out * out)):
            parts[n] = parts[n] + tiles(product, rows)
    return parts


def krylov_own(place, i0, i1, c, ring, v1, grad, sums, mean, b):
    st = Stencil(place)
    for z in range(Z):
        put(mean, 0, z, 0, (i0[z] + i1[z]) * 0.5)
        put(mean, 0, z, Y, ring[0, z])
        for k in range(3):
            put(b, k, z, 0, c[k, z])
            put(b, k, z, Y, ring[k + 1, z])

    def slab(j, parts):
        for r in range(0, R, 24):
            def grad_to(k, value):
                grad[k, j, r : r + 24] = value

            def put_to(k, value):
                v1[k, j, r : r + 24] = value

            parts = first_step(st, mean, b, j + 1, j + 1, r, grad_to, put_to, parts)
        return tuple(parts)

    parts = lax.fori_loop(0, Z - 2, slab, (jnp.zeros((8, X), F32),) * 3)
    for n in range(3):
        sums[n] = parts[n]


def krylov_near(place, i0, i1, c, ring, outer, inner, v1_own, grad_own, own_sums, v1, v2, grad, sums, mean, b):
    st = Stencil(place)
    is_one = lax.rem(st.gz, 2)
    for z in range(Z):
        put(mean, 0, z + 2, 0, (i0[z] + i1[z]) * 0.5)
        put(mean, 0, z + 2, Y, ring[0, z])
        for k in range(3):
            put(b, k, z + 2, 0, c[k, z])
            put(b, k, z + 2, Y, ring[k + 1, z])
    for near, upper in ((inner, 1 - is_one), (outer, is_one)):
        for d in range(2):
            at = jnp.where(upper == 1, Z + 2 + d, 1 - d)
            put(mean, 0, at, 0, near[d])
            for k in range(3):
                put(b, k, at, 0, near[2 + 2 * k + d])
    for k in range(3):
        for j in range(Z - 2):
            put(v1, k, j + 2, 0, v1_own[k, j])
            grad[k, j + 2] = grad_own[k, j]

    zero = jnp.zeros((8, X), F32)

    def first(j, carry):
        z = jnp.where(j < 2, j - 1, j + Z - 3)
        mine = jnp.where((z >= 0) & (z < Z), 1.0, 0.0)
        parts = [zero] * 3
        for r in range(0, R, 24):
            def grad_to(k, value):
                grad[k, z + 1, r : r + 24] = value

            def put_to(k, value):
                put(v1, k, z + 1, r, value)

            parts = first_step(st, mean, b, z + 2, z, r, grad_to, put_to, parts)
        return tuple(m + mine * t for m, t in zip(carry, parts))

    m0, m1, m2 = lax.fori_loop(0, 4, first, tuple(own_sums[n] for n in range(3)))

    def second(z, carry):
        m3, m4 = carry
        for r in range(0, R, 24):
            rows = 24 if r < R - 24 else 16
            g = [grad[k, z + 1, r : r + 24] for k in range(3)]
            vs, totals = [], []
            for k in range(3):
                v, total = flat(v1, k, z + 1, r)
                vs.append(v)
                totals.append(total + (v1[k, z, 8 + r : 32 + r] + v1[k, z + 2, 8 + r : 32 + r]))
            for k, image in enumerate(apply(g, vs, totals)):
                out = st.mask(image, z, r)
                put(v2, k, z + 1, r, out)
                m3 = m3 + tiles(vs[k] * out, rows)
                m4 = m4 + tiles(out * out, rows)
        return m3, m4

    m3, m4 = lax.fori_loop(0, Z, second, (zero,) * 2)

    def third(z, m5):
        low = jnp.where(z > 0, 1.0, 0.0)
        for r in range(0, R, 24):
            rows = 24 if r < R - 24 else 16
            dot = 0.0
            for k in range(3):
                v, total = flat(v2, k, z + 1, r)
                dot = dot + grad[k, z + 1, r : r + 24] * v
                below = v2[k, jnp.maximum(z, 1), 8 + r : 32 + r] * low
                m5 = m5 + tiles(v * (3.0 * v - 0.5 * total - below), rows)
            m5 = m5 + tiles(dot * dot, rows)
        return m5

    m5 = lax.fori_loop(0, Z, third, zero)
    for n, m in enumerate((m0, m1, m2, m3, m4, m5)):
        sums[n] = m


def krylov_far(place, outer, inner, outer_far, inner_far, v1, v2, grad, near_sums, v2_far, b_far, late, sums, mean, b, v1_far):
    st = Stencil(place)
    is_one = lax.rem(st.gz, 2)
    for near, far, side in ((inner, inner_far, 1 - is_one), (outer, outer_far, is_one)):
        put(mean, 0, side, 0, near[1])
        mean[1, side, 0:R] = near[0]
        mean[2, side, 0:R] = far[0]
        for k in range(3):
            put(b, k, side, 0, near[3 + 2 * k])
            b[3 + k, side, 0:R] = near[2 + 2 * k]
            b[6 + k, side, 0:R] = far[1 + k]
            b_far[k, side] = near[2 + 2 * k, 0:Y]
        for k in range(2):
            late[side, k] = far[4 + k, 0:Y]
    cross = jnp.zeros((8, X), F32)
    for side, z2, z1, edge in ((0, -2, -1, 0), (1, Z + 1, Z, Z - 1)):
        for r in range(0, R, 24):
            before, after = (2, 1) if side == 0 else (1, 2)
            g = gradient(
                mean[before, side, r : r + 24],
                mean[after, side, r : r + 24],
                mean[0, side, 8 + r : 32 + r],
                *row_sides(mean, 0, side, r),
            )
            vs, totals = [], []
            for k in range(3):
                v, total = flat(b, k, side, r)
                vs.append(v)
                totals.append(total + (b[3 + k, side, r : r + 24] + b[6 + k, side, r : r + 24]))
            for k, image in enumerate(apply(g, vs, totals)):
                v1_far[k, side, r : r + 24] = st.mask(image, z2, r)
        for r in range(0, R, 24):
            rows = 24 if r < R - 24 else 16
            g = [grad[k, z1 + 1, r : r + 24] for k in range(3)]
            vs, totals = [], []
            for k in range(3):
                v, total = flat(v1, k, z1 + 1, r)
                vs.append(v)
                totals.append(total + (v1_far[k, side, r : r + 24] + v1[k, edge + 1, 8 + r : 32 + r]))
            for k, image in enumerate(apply(g, vs, totals)):
                out = st.mask(image, z1, r)
                v2_far[k, side, r : r + 24] = out
                cross = cross + tiles(v2[k, edge + 1, 8 + r : 32 + r] * out, rows)
    lane = lax.broadcasted_iota(jnp.int32, sums.shape, 1)
    out = jnp.zeros(sums.shape, F32)
    for n in range(6):
        m = near_sums[n] - 0.5 * cross if n == 5 else near_sums[n]
        out = jnp.where(lane == n, jnp.sum(m), out)
    sums[...] = out


def finish(
    sums, c, ring, v1, v2, b_far, v2_far, grad, i0, i1, f, late_rows, late, adj_out, out0_out, out1_out,
    adj, out0, out1, c0, c1, c2, sems,
):
    total = jnp.sum(sums[...], axis=0, keepdims=True)
    m = [total[0, k] for k in range(6)]
    a0 = m[0] / m[1]
    rr1 = m[0] - 2.0 * a0 * m[1] + a0 * a0 * m[2]
    b0 = rr1 / m[0]
    p10, p11 = 1.0 + b0, -a0
    a1 = rr1 / (p10 * p10 * m[1] + 2.0 * p10 * p11 * m[2] + p11 * p11 * m[3])
    r21, r22 = -a0 - a1 * p10, -a1 * p11
    rr2 = m[0] + r21 * r21 * m[2] + r22 * r22 * m[4] + 2.0 * (r21 * m[1] + r22 * m[2] + r21 * r22 * m[3])
    b1 = rr2 / rr1
    p20, p21, p22 = 1.0 + b1 * p10, r21 + b1 * p11, r22
    a2 = rr2 / (
        p20 * p20 * m[1] + p21 * p21 * m[3] + p22 * p22 * m[5]
        + 2.0 * (p20 * p21 * m[2] + p20 * p22 * m[3] + p21 * p22 * m[4])
    )
    w0 = a0 + a1 * p10 + a2 * p20
    w1 = a1 * p11 + a2 * p21
    w2 = a2 * p22

    def combine(z, lo, hi, start, last):
        a = [
            w0 * start(k) + w1 * v1[k, z + 1, 8 + lo : 8 + hi] + w2 * last(k)
            for k in range(3)
        ]
        g = [grad[k, z + 1, lo:hi] for k in range(3)]
        return a, g, g[0] * a[0] + g[1] * a[1] + g[2] * a[2]

    for side, z in ((0, -1), (1, Z)):
        a, g, along = combine(z, 0, Y, lambda k: b_far[k, side], lambda k: v2_far[k, side, 0:Y])
        c0[z + 1] = -a[0] * (g[0] * late[side, 1] + late[side, 0]) - late[side, 1] * along

    copies = []

    def send(n, source, target):
        copies.append(pltpu.make_async_copy(source, target, sems.at[n]))
        copies[-1].start()

    def coupling(z):
        a, g, along = combine(z, 0, Y, lambda k: c[k, z], lambda k: v2[k, z + 1, 8 : 8 + Y])
        fl = [f[k, z] for k in range(3)]
        rest = g[0] * fl[0] + g[1] * fl[1] + g[2] * fl[2] + (i1[z] - i0[z])
        for k in range(3):
            adj[k, z] = a[k]
        send(z, adj.at[:, z], adj_out.at[:, z])
        c0[z + 1] = -a[0] * rest - fl[0] * along
        c1[z, 8 : 8 + Y] = -a[1] * rest - fl[1] * along
        c2[z] = -a[2] * rest - fl[2] * along
        out0[z] = along
        a, g, along = combine(z, Y, R, lambda k: ring[k + 1, z], lambda k: v2[k, z + 1, 8 + Y : 8 + R])
        rows = [late_rows[k, z] for k in range(4)]
        rest = g[0] * rows[1] + g[1] * rows[2] + g[2] * rows[3] + rows[0]
        side = -a[1] * rest - rows[2] * along
        c1[z, 0:8] = side
        c1[z, 8 + Y : 16 + Y] = side

    def spread(z):
        left, right = lane_sides(c2[z])
        total = (c0[z + 2] - c0[z]) + (c1[z, 9 : 9 + Y] - c1[z, 7 : 7 + Y]) + (right - left)
        half = total * -0.25
        along = out0[z]
        out0[z] = half + along
        out1[z] = half - along
        send(Z + z, out0.at[z], out0_out.at[z])
        send(2 * Z + z, out1.at[z], out1_out.at[z])

    coupling(0)
    for z in range(1, Z):
        coupling(z)
        spread(z - 1)
    spread(Z - 1)
    for copy in copies:
        copy.wait()


def vmem(*dims):
    return pltpu.VMEM(dims, F32)


def pinned(array):
    return pltpu.with_memory_space_constraint(array, pltpu.VMEM)


def hbm(*arrays):
    return [pltpu.with_memory_space_constraint(array, pltpu.HBM) for array in arrays]


def shape(*dims):
    return jax.ShapeDtypeStruct(dims, F32)


def shards(image0, image1, flow, cotangent):
    gz, gy = lax.axis_index("gz"), lax.axis_index("gy")
    nz, ny = lax.axis_size("gz"), lax.axis_size("gy")
    place = jnp.stack([gz, gy, jnp.int32(nz), jnp.int32(ny)]).astype(jnp.int32)
    devices = nz * ny

    side, middle = pl.pallas_call(
        pack_rows,
        in_specs=[SM] + [HB] * 4,
        out_specs=[VM] * 2,
        out_shape=[vmem(2, Z, 8, X)] * 2,
        scratch_shapes=[
            pltpu.VMEM((2, Z, 8, X), F32),
            pltpu.VMEM((2, Z, 8, X), F32),
            pltpu.VMEM((2, 3, Z, 8, X), F32),
            pltpu.VMEM((2, 3, Z, 8, X), F32),
            pltpu.SemaphoreType.DMA((2, 4)),
        ],
        compiler_params=params(8),
        name="pack_rows",
    )(place, *hbm(image0, image1, cotangent, flow))

    def swaps(count, start):
        pairs = [(i, i + 1) for i in range(start, count - 1, 2)]
        return pairs + [(j, i) for i, j in pairs]

    middle = lax.ppermute(middle, "gy", swaps(ny, 1))
    side = lax.ppermute(side, "gy", swaps(ny, 0))

    ring, late_rows, inner, outer, inner_far, outer_far = pl.pallas_call(
        pack_slabs,
        in_specs=[SM] + [VM] * 6,
        out_specs=[VM] * 6,
        out_shape=[vmem(4, Z, 8, X)] * 2 + [vmem(8, R, X)] * 2 + [vmem(6, R, X)] * 2,
        compiler_params=params(8),
        name="pack_slabs",
    )(place, image0, image1, cotangent, flow, pinned(middle), pinned(side))
    inner = lax.ppermute(inner, "gz", swaps(nz, 0))
    outer = lax.ppermute(outer, "gz", swaps(nz, 1))
    outer_far = lax.ppermute(outer_far, "gz", swaps(nz, 1))
    inner_far = lax.ppermute(inner_far, "gz", swaps(nz, 0))
    inner, outer = pinned(inner), pinned(outer)

    v1_own, grad_own, own_sums = pl.pallas_call(
        krylov_own,
        in_specs=[SM] + [VM] * 4,
        out_specs=[VM] * 3,
        out_shape=[vmem(3, Z - 2, R, X), vmem(3, Z - 2, R, X), vmem(3, 8, X)],
        scratch_shapes=[pltpu.VMEM((1, Z, PAD, X), F32), pltpu.VMEM((3, Z, PAD, X), F32)],
        compiler_params=params(12),
        name="krylov_own",
    )(place, image0, image1, cotangent, ring)

    v1, v2, grad, near_sums = pl.pallas_call(
        krylov_near,
        in_specs=[SM] + [VM] * 9,
        out_specs=[VM] * 4,
        out_shape=[vmem(3, Z + 2, PAD, X), vmem(3, Z + 2, PAD, X), vmem(3, Z + 2, R, X), vmem(6, 8, X)],
        scratch_shapes=[pltpu.VMEM((1, Z + 4, PAD, X), F32), pltpu.VMEM((3, Z + 4, PAD, X), F32)],
        compiler_params=params(16),
        name="krylov_near",
    )(place, image0, image1, cotangent, ring, outer, inner, v1_own, grad_own, own_sums)

    v2_far, b_far, late, sums = pl.pallas_call(
        krylov_far,
        in_specs=[SM] + [VM] * 8,
        out_specs=[VM] * 4,
        out_shape=[vmem(3, 2, R, X), vmem(3, 2, Y, X), vmem(2, 2, Y, X), vmem(devices, 128)],
        scratch_shapes=[
            pltpu.VMEM((3, 2, PAD, X), F32),
            pltpu.VMEM((9, 2, PAD, X), F32),
            pltpu.VMEM((3, 2, R, X), F32),
        ],
        compiler_params=params(12),
        name="krylov_far",
    )(place, outer, inner, pinned(outer_far), pinned(inner_far), v1, v2, grad, near_sums)

    sums = lax.all_to_all(sums.reshape(devices, 1, 128), ("gz", "gy"), 0, 0).reshape(devices, 128)

    return pl.pallas_call(
        finish,
        in_specs=[VM] * 13,
        out_specs=[HB] * 3,
        out_shape=[shape(3, Z, Y, X), shape(Z, Y, X), shape(Z, Y, X)],
        scratch_shapes=[
            pltpu.VMEM((3, Z, Y, X), F32),
            pltpu.VMEM((Z, Y, X), F32),
            pltpu.VMEM((Z, Y, X), F32),
            pltpu.VMEM((Z + 2, Y, X), F32),
            pltpu.VMEM((Z, Y + 16, X), F32),
            pltpu.VMEM((Z, Y, X), F32),
            pltpu.SemaphoreType.DMA((3 * Z,)),
        ],
        compiler_params=params(12),
        name="finish",
    )(sums, cotangent, ring, v1, v2, b_far, v2_far, grad, image0, image1, flow, late_rows, late)


def solution(mesh):
    return jax.shard_map(
        shards,
        mesh=mesh,
        in_specs=(
            P("gz", "gy", None),
            P("gz", "gy", None),
            P(None, "gz", "gy", None),
            P(None, "gz", "gy", None),
        ),
        out_specs=(P(None, "gz", "gy", None), P("gz", "gy", None), P("gz", "gy", None)),
        check_vma=False,
    )
```

```python
import functools

import jax
import jax.numpy as jnp
from jax import lax
from jax.experimental import pallas as pl
from jax.experimental.pallas import tpu as pltpu
from jax.sharding import PartitionSpec as P

Z, Y, X = 4, 64, 256
H = X // 2
R = Y + 8
PAD = R + 16
F32 = jnp.float32
VM = pl.BlockSpec(memory_space=pltpu.VMEM)
SM = pl.BlockSpec(memory_space=pltpu.SMEM)
HB = pl.BlockSpec(memory_space=pltpu.HBM)


def params(mib):
    return pltpu.CompilerParams(vmem_limit_bytes=mib * 1024 * 1024)


def lane_sides(v):
    lane = lax.broadcasted_iota(jnp.int32, v.shape[:-1] + (H,), v.ndim - 1)
    first, last = lane == 0, lane == H - 1
    a, b = v[..., :H], v[..., H:]
    ra, rb = pltpu.roll(a, 1, v.ndim - 1), pltpu.roll(b, 1, v.ndim - 1)
    qa, qb = pltpu.roll(a, H - 1, v.ndim - 1), pltpu.roll(b, H - 1, v.ndim - 1)
    left = jnp.concatenate([jnp.where(first, 0.0, ra), jnp.where(first, ra, rb)], axis=-1)
    right = jnp.concatenate([jnp.where(last, qb, qa), jnp.where(last, 0.0, qb)], axis=-1)
    return left, right


def pack_rows(place, i0, i1, c, f, side, middle, t0, t1, tc, tf, sems):
    copies = []
    for s, lo in enumerate((0, Y - 8)):
        rows = pl.ds(lo, 8)
        for n, (src, dst) in enumerate(((i0, t0), (i1, t1))):
            copies.append(pltpu.make_async_copy(src.at[:, rows], dst.at[s], sems.at[s, n]))
        for n, (src, dst) in enumerate(((c, tc), (f, tf))):
            copies.append(pltpu.make_async_copy(src.at[:, :, rows], dst.at[s], sems.at[s, n + 2]))
    for copy in copies:
        copy.start()
    for copy in copies:
        copy.wait()
    odd = lax.rem(place[1], 2) == 1
    sub = lax.broadcasted_iota(jnp.int32, (8, X), 0)

    def roll(v, n):
        return pltpu.roll(v, n, 0)

    for z in range(Z):
        messages = []
        for s in range(2):
            fields = [(t0[s, z] + t1[s, z]) * 0.5] + [tc[s, k, z] for k in range(3)]
            late = [t1[s, z] - t0[s, z]] + [tf[s, k, z] for k in range(3)]
            for p in range(2):
                one, two, one_late, two_late = fields[2 * p], fields[2 * p + 1], late[2 * p], late[2 * p + 1]
                if s == 0:
                    low, high, third, fourth = one, roll(two, 5), roll(one_late, 3), roll(two_late, 4)
                else:
                    low, high, third, fourth = roll(two, 3), one, roll(one_late, 4), roll(two_late, 5)
                messages.append(
                    jnp.where(sub < 3, low, jnp.where(sub == 3, third, jnp.where(sub == 4, fourth, high)))
                )
        for p in range(2):
            down, up = messages[p], messages[2 + p]
            side[p, z] = jnp.where(odd, down, up)
            middle[p, z] = jnp.where(odd, up, down)


def pack_slabs(place, i0, i1, c, middle, side, ring, late_rows, inner, outer):
    is_one = lax.rem(place[0], 2)
    odd = lax.rem(place[1], 2) == 1
    sub = lax.broadcasted_iota(jnp.int32, (8, X), 0)

    def roll(v, n):
        return pltpu.roll(v, n, 0)

    for z in range(Z):
        for p in range(2):
            a = jnp.where(odd, middle[p, z], side[p, z])
            b = jnp.where(odd, side[p, z], middle[p, z])
            ring[2 * p, z] = jnp.where(sub < 3, a, jnp.where(sub >= 5, b, 0.0))
            ring[2 * p + 1, z] = jnp.where(sub < 3, roll(a, 3), jnp.where(sub >= 5, roll(b, 5), 0.0))
            late_rows[2 * p, z] = jnp.where(sub == 0, roll(a, 5), roll(b, 4))
            late_rows[2 * p + 1, z] = jnp.where(sub == 0, roll(a, 4), roll(b, 3))
    for near, first, step in (
        (inner, (Z - 1) * (1 - is_one), 2 * is_one - 1),
        (outer, (Z - 1) * is_one, 1 - 2 * is_one),
    ):
        for d in range(2):
            z = first + d * step
            for k in range(4):
                near[2 * k + d, 0:Y] = c[k - 1, z] if k else (i0[z] + i1[z]) * 0.5
                near[2 * k + d, Y:R] = ring[k, z]


class Stencil:
    def __init__(self, place):
        self.gz, gy, self.nz, ny = (place[n] for n in range(4))
        row = lax.broadcasted_iota(jnp.int32, (24, X), 0) + (R - 24)
        after = jnp.where(gy < ny - 1, 1.0, 0.0)
        before = jnp.where(gy > 0, 1.0, 0.0)
        self.keep = jnp.where(row < Y, 1.0, jnp.where(row < Y + 4, after, before))

    def inside(self, z):
        slab = self.gz * Z + z
        return jnp.where((slab >= 0) & (slab < self.nz * Z), 1.0, 0.0)

    def mask(self, value, z, r):
        value = value * self.inside(z)
        return value * self.keep if r == R - 24 else value


def tiles(value, rows):
    total = value[0:8]
    for r in range(8, rows, 8):
        total = total + value[r : r + 8]
    return total


def put(ref, k, z, r, value):
    rows = value.shape[0]
    ref[k, z, 8 + r : 8 + r + rows] = value
    if r == 0:
        ref[k, z, 8 + R : PAD] = value[0:8]
    if r + rows == R:
        ref[k, z, 0:8] = value[rows - 8 : rows]


def row_sides(ref, k, z, r, rows=24):
    return ref[k, z, 7 + r : 7 + r + rows], ref[k, z, 9 + r : 9 + r + rows]


def apply(g, vs, sums):
    dot = g[0] * vs[0] + g[1] * vs[1] + g[2] * vs[2]
    return [g[k] * dot + (3.0 * vs[k] - 0.5 * sums[k]) for k in range(3)]


def flat(ref, k, z, r, rows=24):
    v = ref[k, z, 8 + r : 8 + r + rows]
    left, right = lane_sides(v)
    before, after = row_sides(ref, k, z, r, rows)
    return v, (before + after) + (left + right)


def first_step(st, mean, b, v1, grad, z, r, parts):
    at = z + 2
    rows = 24 if r < R - 24 else 16
    mid = slice(8 + r, 32 + r)
    left, right = lane_sides(mean[0, at, mid])
    before, after = row_sides(mean, 0, at, r)
    g = [(mean[0, at + 1, mid] - mean[0, at - 1, mid]) * 0.5, (after - before) * 0.5, (right - left) * 0.5]
    vs, totals = [], []
    for k in range(3):
        grad[k, z + 1, r : r + 24] = g[k]
        v, total = flat(b, k, at, r)
        vs.append(v)
        totals.append(total + (b[k, at - 1, mid] + b[k, at + 1, mid]))
    parts = list(parts)
    for k, image in enumerate(apply(g, vs, totals)):
        out = st.mask(image, z, r)
        put(v1, k, z + 1, r, out)
        for n, product in enumerate((vs[k] * vs[k], vs[k] * out, out * out)):
            parts[n] = parts[n] + tiles(product, rows)
    return parts


def krylov_own(place, i0, i1, c, f, ring, mean, b, v1, grad, sums, inner_far, outer_far):
    st = Stencil(place)
    is_one = lax.rem(st.gz, 2)
    for z in range(Z):
        put(mean, 0, z + 2, 0, (i0[z] + i1[z]) * 0.5)
        put(mean, 0, z + 2, Y, ring[0, z])
        for k in range(3):
            put(b, k, z + 2, 0, c[k, z])
            put(b, k, z + 2, Y, ring[k + 1, z])

    def slab(j, parts):
        for r in range(0, R, 24):
            parts = first_step(st, mean, b, v1, grad, j + 1, r, parts)
        return tuple(parts)

    parts = lax.fori_loop(0, Z - 2, slab, (jnp.zeros((8, X), F32),) * 3)
    for n in range(3):
        sums[n] = parts[n]
    for far, first, second in (
        (inner_far, (Z - 1) * (1 - is_one), Z - 2 + is_one * (3 - Z)),
        (outer_far, (Z - 1) * is_one, 1 + is_one * (Z - 3)),
    ):
        for k in range(3):
            far[k] = v1[k, second + 1, 8 : 8 + Y]
        left, right = lane_sides(mean[0, first + 2, 8 : 8 + Y])
        before, after = row_sides(mean, 0, first + 2, 0, Y)
        far[3] = ((after - before) * f[1, first] + (right - left) * f[2, first]) * 0.5 + (i1[first] - i0[first])
        far[4] = f[0, first]


def krylov_near(place, outer, inner, mean_in, b_in, v1_in, grad_in, own_sums, mean, b, v1, grad, v2, sums):
    del mean_in, b_in, v1_in, grad_in
    st = Stencil(place)
    is_one = lax.rem(st.gz, 2)
    for near, upper in ((inner, 1 - is_one), (outer, is_one)):
        for d in range(2):
            at = jnp.where(upper == 1, Z + 2 + d, 1 - d)
            put(mean, 0, at, 0, near[d])
            for k in range(3):
                put(b, k, at, 0, near[2 + 2 * k + d])

    zero = jnp.zeros((8, X), F32)

    def first(j, carry):
        z = jnp.where(j < 2, j - 1, j + Z - 3)
        mine = jnp.where((z >= 0) & (z < Z), 1.0, 0.0)
        parts = [zero] * 3
        for r in range(0, R, 24):
            parts = first_step(st, mean, b, v1, grad, z, r, parts)
        return tuple(m + mine * t for m, t in zip(carry, parts))

    m0, m1, m2 = lax.fori_loop(0, 4, first, tuple(own_sums[n] for n in range(3)))

    def second(z, carry):
        m3, m4 = carry
        for r in range(0, R, 24):
            rows = 24 if r < R - 24 else 16
            g = [grad[k, z + 1, r : r + 24] for k in range(3)]
            vs, totals = [], []
            for k in range(3):
                v, total = flat(v1, k, z + 1, r)
                vs.append(v)
                totals.append(total + (v1[k, z, 8 + r : 32 + r] + v1[k, z + 2, 8 + r : 32 + r]))
            for k, image in enumerate(apply(g, vs, totals)):
                out = st.mask(image, z, r)
                put(v2, k, z + 1, r, out)
                m3 = m3 + tiles(vs[k] * out, rows)
                m4 = m4 + tiles(out * out, rows)
        return m3, m4

    m3, m4 = lax.fori_loop(0, Z, second, (zero,) * 2)

    def third(z, m5):
        low = jnp.where(z > 0, 1.0, 0.0)
        for r in range(0, R, 24):
            rows = 24 if r < R - 24 else 16
            dot = 0.0
            for k in range(3):
                v, total = flat(v2, k, z + 1, r)
                dot = dot + grad[k, z + 1, r : r + 24] * v
                below = v2[k, jnp.maximum(z, 1), 8 + r : 32 + r] * low
                m5 = m5 + tiles(v * (3.0 * v - 0.5 * total - below), rows)
            m5 = m5 + tiles(dot * dot, rows)
        return m5

    m5 = lax.fori_loop(0, Z, third, zero)
    for n, m in enumerate((m0, m1, m2, m3, m4, m5)):
        sums[n] = m


def krylov_far(place, outer_far, inner_far, v1, v2, grad, near_sums, v2_far, late, sums):
    st = Stencil(place)
    is_one = lax.rem(st.gz, 2)

    def face(far, side, cross):
        z = jnp.where(side == 1, Z, -1)
        edge = jnp.where(side == 1, Z, 1)
        scale = st.inside(z)
        for k in range(2):
            late[side, k] = far[3 + k]
        for r in range(0, Y, 16):
            g = [grad[k, z + 1, r : r + 16] for k in range(3)]
            vs, totals = [], []
            for k in range(3):
                v, total = flat(v1, k, z + 1, r, 16)
                vs.append(v)
                totals.append(total + (far[k, r : r + 16] + v1[k, edge, 8 + r : 24 + r]))
            for k, image in enumerate(apply(g, vs, totals)):
                out = image * scale
                v2_far[k, side, r : r + 16] = out
                cross = cross + tiles(v2[k, edge, 8 + r : 24 + r] * out, 16)
        return cross

    cross = face(inner_far, 1 - is_one, jnp.zeros((8, X), F32))
    cross = face(outer_far, is_one, cross)
    lane = lax.broadcasted_iota(jnp.int32, sums.shape, 1)
    out = jnp.zeros(sums.shape, F32)
    for n in range(6):
        m = near_sums[n] - 0.5 * cross if n == 5 else near_sums[n]
        out = jnp.where(lane == n, jnp.sum(m), out)
    sums[...] = out


def finish(
    sums, b, v1, v2, v2_far, grad, i0, i1, f, late_rows, late, adj_out, out0_out, out1_out,
    adj, out0, out1, c0, c1, c2, sems,
):
    total = jnp.sum(sums[...], axis=0, keepdims=True)
    m = [total[0, k] for k in range(6)]
    a0 = m[0] / m[1]
    rr1 = m[0] - 2.0 * a0 * m[1] + a0 * a0 * m[2]
    b0 = rr1 / m[0]
    p10, p11 = 1.0 + b0, -a0
    a1 = rr1 / (p10 * p10 * m[1] + 2.0 * p10 * p11 * m[2] + p11 * p11 * m[3])
    r21, r22 = -a0 - a1 * p10, -a1 * p11
    rr2 = m[0] + r21 * r21 * m[2] + r22 * r22 * m[4] + 2.0 * (r21 * m[1] + r22 * m[2] + r21 * r22 * m[3])
    b1 = rr2 / rr1
    p20, p21, p22 = 1.0 + b1 * p10, r21 + b1 * p11, r22
    a2 = rr2 / (
        p20 * p20 * m[1] + p21 * p21 * m[3] + p22 * p22 * m[5]
        + 2.0 * (p20 * p21 * m[2] + p20 * p22 * m[3] + p21 * p22 * m[4])
    )
    w0 = a0 + a1 * p10 + a2 * p20
    w1 = a1 * p11 + a2 * p21
    w2 = a2 * p22

    def combine(z, lo, hi, last):
        a = [
            w0 * b[k, z + 2, 8 + lo : 8 + hi] + w1 * v1[k, z + 1, 8 + lo : 8 + hi] + w2 * last(k)
            for k in range(3)
        ]
        g = [grad[k, z + 1, lo:hi] for k in range(3)]
        return a, g, g[0] * a[0] + g[1] * a[1] + g[2] * a[2]

    for side, z in ((0, -1), (1, Z)):
        a, g, along = combine(z, 0, Y, lambda k: v2_far[k, side])
        c0[z + 1] = -a[0] * (g[0] * late[side, 1] + late[side, 0]) - late[side, 1] * along

    copies = []

    def send(n, source, target):
        copies.append(pltpu.make_async_copy(source, target, sems.at[n]))
        copies[-1].start()

    def coupling(z):
        a, g, along = combine(z, 0, Y, lambda k: v2[k, z + 1, 8 : 8 + Y])
        fl = [f[k, z] for k in range(3)]
        rest = g[0] * fl[0] + g[1] * fl[1] + g[2] * fl[2] + (i1[z] - i0[z])
        for k in range(3):
            adj[k, z] = a[k]
        send(z, adj.at[:, z], adj_out.at[:, z])
        c0[z + 1] = -a[0] * rest - fl[0] * along
        c1[z, 8 : 8 + Y] = -a[1] * rest - fl[1] * along
        c2[z] = -a[2] * rest - fl[2] * along
        out0[z] = along
        a, g, along = combine(z, Y, R, lambda k: v2[k, z + 1, 8 + Y : 8 + R])
        rows = [late_rows[k, z] for k in range(4)]
        rest = g[0] * rows[1] + g[1] * rows[2] + g[2] * rows[3] + rows[0]
        side = -a[1] * rest - rows[2] * along
        c1[z, 0:8] = side
        c1[z, 8 + Y : 16 + Y] = side

    def spread(z):
        left, right = lane_sides(c2[z])
        total = (c0[z + 2] - c0[z]) + (c1[z, 9 : 9 + Y] - c1[z, 7 : 7 + Y]) + (right - left)
        half = total * -0.25
        along = out0[z]
        out0[z] = half + along
        out1[z] = half - along
        send(Z + z, out0.at[z], out0_out.at[z])
        send(2 * Z + z, out1.at[z], out1_out.at[z])

    coupling(0)
    for z in range(1, Z):
        coupling(z)
        spread(z - 1)
    spread(Z - 1)
    for copy in copies:
        copy.wait()


def vmem(*dims):
    return pltpu.VMEM(dims, F32)


def pinned(array):
    return pltpu.with_memory_space_constraint(array, pltpu.VMEM)


def hbm(*arrays):
    return [pltpu.with_memory_space_constraint(array, pltpu.HBM) for array in arrays]


def shape(*dims):
    return jax.ShapeDtypeStruct(dims, F32)


def shards(image0, image1, flow, cotangent):
    gz, gy = lax.axis_index("gz"), lax.axis_index("gy")
    nz, ny = lax.axis_size("gz"), lax.axis_size("gy")
    place = jnp.stack([gz, gy, jnp.int32(nz), jnp.int32(ny)]).astype(jnp.int32)
    devices = nz * ny

    side, middle = pl.pallas_call(
        pack_rows,
        in_specs=[SM] + [HB] * 4,
        out_specs=[VM] * 2,
        out_shape=[vmem(2, Z, 8, X)] * 2,
        scratch_shapes=[
            pltpu.VMEM((2, Z, 8, X), F32),
            pltpu.VMEM((2, Z, 8, X), F32),
            pltpu.VMEM((2, 3, Z, 8, X), F32),
            pltpu.VMEM((2, 3, Z, 8, X), F32),
            pltpu.SemaphoreType.DMA((2, 4)),
        ],
        compiler_params=params(8),
        name="pack_rows",
    )(place, *hbm(image0, image1, cotangent, flow))

    def swaps(count, start):
        pairs = [(i, i + 1) for i in range(start, count - 1, 2)]
        return pairs + [(j, i) for i, j in pairs]

    middle = lax.ppermute(middle, "gy", swaps(ny, 1))
    side = lax.ppermute(side, "gy", swaps(ny, 0))

    ring, late_rows, inner, outer = pl.pallas_call(
        pack_slabs,
        in_specs=[SM] + [VM] * 5,
        out_specs=[VM] * 4,
        out_shape=[vmem(4, Z, 8, X)] * 2 + [vmem(8, R, X)] * 2,
        compiler_params=params(8),
        name="pack_slabs",
    )(place, image0, image1, cotangent, pinned(middle), pinned(side))
    outer = lax.ppermute(outer, "gz", swaps(nz, 1))
    inner = lax.ppermute(inner, "gz", swaps(nz, 0))

    fields = [vmem(1, Z + 4, PAD, X), vmem(3, Z + 4, PAD, X), vmem(3, Z + 2, PAD, X), vmem(3, Z + 2, R, X)]
    *fields_own, own_sums, inner_far, outer_far = pl.pallas_call(
        krylov_own,
        in_specs=[SM] + [VM] * 5,
        out_specs=[VM] * 7,
        out_shape=fields + [vmem(3, 8, X), vmem(5, Y, X), vmem(5, Y, X)],
        compiler_params=params(12),
        name="krylov_own",
    )(place, image0, image1, cotangent, flow, ring)
    outer_far = lax.ppermute(outer_far, "gz", swaps(nz, 1))
    inner_far = lax.ppermute(inner_far, "gz", swaps(nz, 0))

    _, b, v1, grad, v2, near_sums = pl.pallas_call(
        krylov_near,
        in_specs=[SM] + [VM] * 7,
        out_specs=[VM] * 6,
        out_shape=fields + [vmem(3, Z + 2, PAD, X), vmem(6, 8, X)],
        input_output_aliases={3 + n: n for n in range(4)},
        compiler_params=params(12),
        name="krylov_near",
    )(place, pinned(outer), pinned(inner), *fields_own, own_sums)

    v2_far, late, sums = pl.pallas_call(
        krylov_far,
        in_specs=[SM] + [VM] * 6,
        out_specs=[VM] * 3,
        out_shape=[vmem(3, 2, Y, X), vmem(2, 2, Y, X), vmem(devices, 128)],
        compiler_params=params(12),
        name="krylov_far",
    )(place, pinned(outer_far), pinned(inner_far), v1, v2, grad, near_sums)

    sums = lax.all_to_all(sums.reshape(devices, 1, 128), ("gz", "gy"), 0, 0).reshape(devices, 128)

    return pl.pallas_call(
        finish,
        in_specs=[VM] * 11,
        out_specs=[HB] * 3,
        out_shape=[shape(3, Z, Y, X), shape(Z, Y, X), shape(Z, Y, X)],
        scratch_shapes=[
            pltpu.VMEM((3, Z, Y, X), F32),
            pltpu.VMEM((Z, Y, X), F32),
            pltpu.VMEM((Z, Y, X), F32),
            pltpu.VMEM((Z + 2, Y, X), F32),
            pltpu.VMEM((Z, Y + 16, X), F32),
            pltpu.VMEM((Z, Y, X), F32),
            pltpu.SemaphoreType.DMA((3 * Z,)),
        ],
        compiler_params=params(12),
        name="finish",
    )(sums, b, v1, v2, v2_far, grad, image0, image1, flow, late_rows, late)


def solution(mesh):
    return jax.shard_map(
        shards,
        mesh=mesh,
        in_specs=(
            P("gz", "gy", None),
            P("gz", "gy", None),
            P(None, "gz", "gy", None),
            P(None, "gz", "gy", None),
        ),
        out_specs=(P(None, "gz", "gy", None), P("gz", "gy", None), P("gz", "gy", None)),
        check_vma=False,
    )
```

```python
import functools

import jax
import jax.numpy as jnp
from jax import lax
from jax.experimental import pallas as pl
from jax.experimental.pallas import tpu as pltpu
from jax.sharding import PartitionSpec as P

Z, Y, X = 4, 64, 256
H = X // 2
R = Y + 8
PAD = R + 16
F32 = jnp.float32
VM = pl.BlockSpec(memory_space=pltpu.VMEM)
HB = pl.BlockSpec(memory_space=pltpu.HBM)


def params(mib):
    return pltpu.CompilerParams(vmem_limit_bytes=mib * 1024 * 1024)


def lane_sides(v):
    lane = lax.broadcasted_iota(jnp.int32, v.shape[:-1] + (H,), v.ndim - 1)
    first, last = lane == 0, lane == H - 1
    a, b = v[..., :H], v[..., H:]
    ra, rb = pltpu.roll(a, 1, v.ndim - 1), pltpu.roll(b, 1, v.ndim - 1)
    qa, qb = pltpu.roll(a, H - 1, v.ndim - 1), pltpu.roll(b, H - 1, v.ndim - 1)
    left = jnp.concatenate([jnp.where(first, 0.0, ra), jnp.where(first, ra, rb)], axis=-1)
    right = jnp.concatenate([jnp.where(last, qb, qa), jnp.where(last, 0.0, qb)], axis=-1)
    return left, right


def pack_rows(i0, i1, c, f, side, middle, t0, t1, tc, tf, sems):
    copies = []
    for s, lo in enumerate((0, Y - 8)):
        rows = pl.ds(lo, 8)
        for n, (src, dst) in enumerate(((i0, t0), (i1, t1))):
            copies.append(pltpu.make_async_copy(src.at[:, rows], dst.at[s], sems.at[s, n]))
        for n, (src, dst) in enumerate(((c, tc), (f, tf))):
            copies.append(pltpu.make_async_copy(src.at[:, :, rows], dst.at[s], sems.at[s, n + 2]))
    for copy in copies:
        copy.start()
    for copy in copies:
        copy.wait()
    odd = lax.rem(lax.axis_index("gy"), 2) == 1
    sub = lax.broadcasted_iota(jnp.int32, (8, X), 0)

    def roll(v, n):
        return pltpu.roll(v, n, 0)

    for z in range(Z):
        messages = []
        for s in range(2):
            fields = [(t0[s, z] + t1[s, z]) * 0.5] + [tc[s, k, z] for k in range(3)]
            late = [t1[s, z] - t0[s, z]] + [tf[s, k, z] for k in range(3)]
            for p in range(2):
                one, two, one_late, two_late = fields[2 * p], fields[2 * p + 1], late[2 * p], late[2 * p + 1]
                if s == 0:
                    low, high, third, fourth = one, roll(two, 5), roll(one_late, 3), roll(two_late, 4)
                else:
                    low, high, third, fourth = roll(two, 3), one, roll(one_late, 4), roll(two_late, 5)
                messages.append(
                    jnp.where(sub < 3, low, jnp.where(sub == 3, third, jnp.where(sub == 4, fourth, high)))
                )
        for p in range(2):
            down, up = messages[p], messages[2 + p]
            side[p, z] = jnp.where(odd, down, up)
            middle[p, z] = jnp.where(odd, up, down)


def load(i0, i1, c, f, after, mean, b, temporal, flow, t0, t1, sems):
    del after
    copies = [
        pltpu.make_async_copy(i0, t0, sems.at[0]),
        pltpu.make_async_copy(i1, t1, sems.at[1]),
        pltpu.make_async_copy(c, b.at[:, 2 : 2 + Z, 8 : 8 + Y], sems.at[2]),
        pltpu.make_async_copy(f, flow, sems.at[3]),
    ]
    for copy in copies:
        copy.start()
    for copy in copies[:2]:
        copy.wait()
    for z in range(Z):
        put(mean, 0, z + 2, 0, (t0[z] + t1[z]) * 0.5)
        temporal[z] = t1[z] - t0[z]
    copies[2].wait()
    for z in range(Z):
        for k in range(3):
            b[k, z + 2, 8 + R : PAD] = b[k, z + 2, 8:16]
    copies[3].wait()


def pack_slabs(mean, b, middle, side, ring, late_rows, inner, outer):
    is_one = lax.rem(lax.axis_index("gz"), 2)
    odd = lax.rem(lax.axis_index("gy"), 2) == 1
    sub = lax.broadcasted_iota(jnp.int32, (8, X), 0)

    def roll(v, n):
        return pltpu.roll(v, n, 0)

    for z in range(Z):
        for p in range(2):
            a = jnp.where(odd, middle[p, z], side[p, z])
            b_tile = jnp.where(odd, side[p, z], middle[p, z])
            ring[2 * p, z] = jnp.where(sub < 3, a, jnp.where(sub >= 5, b_tile, 0.0))
            ring[2 * p + 1, z] = jnp.where(sub < 3, roll(a, 3), jnp.where(sub >= 5, roll(b_tile, 5), 0.0))
            late_rows[2 * p, z] = jnp.where(sub == 0, roll(a, 5), roll(b_tile, 4))
            late_rows[2 * p + 1, z] = jnp.where(sub == 0, roll(a, 4), roll(b_tile, 3))
    for near, first, step in (
        (inner, (Z - 1) * (1 - is_one), 2 * is_one - 1),
        (outer, (Z - 1) * is_one, 1 - 2 * is_one),
    ):
        for d in range(2):
            z = first + d * step
            for k in range(4):
                source, n = (b, k - 1) if k else (mean, 0)
                near[2 * k + d, 0:Y] = source[n, z + 2, 8 : 8 + Y]
                near[2 * k + d, Y:R] = ring[k, z]


class Stencil:
    def __init__(self):
        self.gz, gy = lax.axis_index("gz"), lax.axis_index("gy")
        self.nz, ny = lax.axis_size("gz"), lax.axis_size("gy")
        row = lax.broadcasted_iota(jnp.int32, (24, X), 0) + (R - 24)
        after = jnp.where(gy < ny - 1, 1.0, 0.0)
        before = jnp.where(gy > 0, 1.0, 0.0)
        self.keep = jnp.where(row < Y, 1.0, jnp.where(row < Y + 4, after, before))

    def inside(self, z):
        slab = self.gz * Z + z
        return jnp.where((slab >= 0) & (slab < self.nz * Z), 1.0, 0.0)

    def mask(self, value, z, r):
        value = value * self.inside(z)
        return value * self.keep if r == R - 24 else value


def tiles(value, rows):
    total = value[0:8]
    for r in range(8, rows, 8):
        total = total + value[r : r + 8]
    return total


def put(ref, k, z, r, value):
    rows = value.shape[0]
    ref[k, z, 8 + r : 8 + r + rows] = value
    if r == 0:
        ref[k, z, 8 + R : PAD] = value[0:8]
    if r + rows == R:
        ref[k, z, 0:8] = value[rows - 8 : rows]


def row_sides(ref, k, z, r, rows=24):
    return ref[k, z, 7 + r : 7 + r + rows], ref[k, z, 9 + r : 9 + r + rows]


def apply(g, vs, sums):
    dot = g[0] * vs[0] + g[1] * vs[1] + g[2] * vs[2]
    return [g[k] * dot + (3.0 * vs[k] - 0.5 * sums[k]) for k in range(3)]


def flat(ref, k, z, r, rows=24):
    v = ref[k, z, 8 + r : 8 + r + rows]
    left, right = lane_sides(v)
    before, after = row_sides(ref, k, z, r, rows)
    return v, (before + after) + (left + right)


def first_step(st, mean, b, v1, grad, z, r, parts):
    at = z + 2
    rows = 24 if r < R - 24 else 16
    mid = slice(8 + r, 32 + r)
    left, right = lane_sides(mean[0, at, mid])
    before, after = row_sides(mean, 0, at, r)
    g = [(mean[0, at + 1, mid] - mean[0, at - 1, mid]) * 0.5, (after - before) * 0.5, (right - left) * 0.5]
    vs, totals = [], []
    for k in range(3):
        grad[k, z + 1, r : r + 24] = g[k]
        v, total = flat(b, k, at, r)
        vs.append(v)
        totals.append(total + (b[k, at - 1, mid] + b[k, at + 1, mid]))
    parts = list(parts)
    for k, image in enumerate(apply(g, vs, totals)):
        out = st.mask(image, z, r)
        put(v1, k, z + 1, r, out)
        for n, product in enumerate((vs[k] * vs[k], vs[k] * out, out * out)):
            parts[n] = parts[n] + tiles(product, rows)
    return parts


def krylov_own(mean_in, b_in, temporal, f, ring, mean, b, v1, grad, sums, inner_far, outer_far):
    del mean_in, b_in
    st = Stencil()
    is_one = lax.rem(st.gz, 2)
    for z in range(Z):
        put(mean, 0, z + 2, Y, ring[0, z])
        for k in range(3):
            put(b, k, z + 2, Y, ring[k + 1, z])

    def slab(j, parts):
        for r in range(0, R, 24):
            parts = first_step(st, mean, b, v1, grad, j + 1, r, parts)
        return tuple(parts)

    parts = lax.fori_loop(0, Z - 2, slab, (jnp.zeros((8, X), F32),) * 3)
    for n in range(3):
        sums[n] = parts[n]
    for far, first, second in (
        (inner_far, (Z - 1) * (1 - is_one), Z - 2 + is_one * (3 - Z)),
        (outer_far, (Z - 1) * is_one, 1 + is_one * (Z - 3)),
    ):
        for k in range(3):
            far[k] = v1[k, second + 1, 8 : 8 + Y]
        left, right = lane_sides(mean[0, first + 2, 8 : 8 + Y])
        before, after = row_sides(mean, 0, first + 2, 0, Y)
        far[3] = ((after - before) * f[1, first] + (right - left) * f[2, first]) * 0.5 + temporal[first]
        far[4] = f[0, first]


def krylov_near(outer, inner, mean_in, b_in, v1_in, grad_in, own_sums, mean, b, v1, grad, v2, sums):
    del mean_in, b_in, v1_in, grad_in
    st = Stencil()
    is_one = lax.rem(st.gz, 2)
    for near, upper in ((inner, 1 - is_one), (outer, is_one)):
        for d in range(2):
            at = jnp.where(upper == 1, Z + 2 + d, 1 - d)
            put(mean, 0, at, 0, near[d])
            for k in range(3):
                put(b, k, at, 0, near[2 + 2 * k + d])

    zero = jnp.zeros((8, X), F32)

    def first(j, carry):
        z = jnp.where(j < 2, j - 1, j + Z - 3)
        mine = jnp.where((z >= 0) & (z < Z), 1.0, 0.0)
        parts = [zero] * 3
        for r in range(0, R, 24):
            parts = first_step(st, mean, b, v1, grad, z, r, parts)
        return tuple(m + mine * t for m, t in zip(carry, parts))

    m0, m1, m2 = lax.fori_loop(0, 4, first, tuple(own_sums[n] for n in range(3)))

    def second(z, carry):
        m3, m4 = carry
        for r in range(0, R, 24):
            rows = 24 if r < R - 24 else 16
            g = [grad[k, z + 1, r : r + 24] for k in range(3)]
            vs, totals = [], []
            for k in range(3):
                v, total = flat(v1, k, z + 1, r)
                vs.append(v)
                totals.append(total + (v1[k, z, 8 + r : 32 + r] + v1[k, z + 2, 8 + r : 32 + r]))
            for k, image in enumerate(apply(g, vs, totals)):
                out = st.mask(image, z, r)
                put(v2, k, z + 1, r, out)
                m3 = m3 + tiles(vs[k] * out, rows)
                m4 = m4 + tiles(out * out, rows)
        return m3, m4

    m3, m4 = lax.fori_loop(0, Z, second, (zero,) * 2)

    def third(z, m5):
        low = jnp.where(z > 0, 1.0, 0.0)
        for r in range(0, R, 24):
            rows = 24 if r < R - 24 else 16
            dot = 0.0
            for k in range(3):
                v, total = flat(v2, k, z + 1, r)
                dot = dot + grad[k, z + 1, r : r + 24] * v
                below = v2[k, jnp.maximum(z, 1), 8 + r : 32 + r] * low
                m5 = m5 + tiles(v * (3.0 * v - 0.5 * total - below), rows)
            m5 = m5 + tiles(dot * dot, rows)
        return m5

    m5 = lax.fori_loop(0, Z, third, zero)
    for n, m in enumerate((m0, m1, m2, m3, m4, m5)):
        sums[n] = m


def krylov_far(outer_far, inner_far, v1, v2, grad, near_sums, v2_far, late, sums):
    st = Stencil()
    is_one = lax.rem(st.gz, 2)

    def face(far, side, cross):
        z = jnp.where(side == 1, Z, -1)
        edge = jnp.where(side == 1, Z, 1)
        scale = st.inside(z)
        for k in range(2):
            late[side, k] = far[3 + k]
        for r in range(0, Y, 16):
            g = [grad[k, z + 1, r : r + 16] for k in range(3)]
            vs, totals = [], []
            for k in range(3):
                v, total = flat(v1, k, z + 1, r, 16)
                vs.append(v)
                totals.append(total + (far[k, r : r + 16] + v1[k, edge, 8 + r : 24 + r]))
            for k, image in enumerate(apply(g, vs, totals)):
                out = image * scale
                v2_far[k, side, r : r + 16] = out
                cross = cross + tiles(v2[k, edge, 8 + r : 24 + r] * out, 16)
        return cross

    cross = face(inner_far, 1 - is_one, jnp.zeros((8, X), F32))
    cross = face(outer_far, is_one, cross)
    lane = lax.broadcasted_iota(jnp.int32, sums.shape, 1)
    out = jnp.zeros(sums.shape, F32)
    for n in range(6):
        m = near_sums[n] - 0.5 * cross if n == 5 else near_sums[n]
        out = jnp.where(lane == n, jnp.sum(m), out)
    sums[...] = out


def finish(
    sums, b, v1, v2, v2_far, grad, temporal, f, late_rows, late, adj_out, out0_out, out1_out,
    adj, out0, out1, c0, c1, c2, sems,
):
    total = jnp.sum(sums[...], axis=0, keepdims=True)
    lane = lax.broadcasted_iota(jnp.int32, total.shape, 1)
    m = [jnp.sum(jnp.where(lane == k, total, 0.0), axis=1, keepdims=True) for k in range(6)]
    a0 = m[0] / m[1]
    rr1 = m[0] - 2.0 * a0 * m[1] + a0 * a0 * m[2]
    b0 = rr1 / m[0]
    p10, p11 = 1.0 + b0, -a0
    a1 = rr1 / (p10 * p10 * m[1] + 2.0 * p10 * p11 * m[2] + p11 * p11 * m[3])
    r21, r22 = -a0 - a1 * p10, -a1 * p11
    rr2 = m[0] + r21 * r21 * m[2] + r22 * r22 * m[4] + 2.0 * (r21 * m[1] + r22 * m[2] + r21 * r22 * m[3])
    b1 = rr2 / rr1
    p20, p21, p22 = 1.0 + b1 * p10, r21 + b1 * p11, r22
    a2 = rr2 / (
        p20 * p20 * m[1] + p21 * p21 * m[3] + p22 * p22 * m[5]
        + 2.0 * (p20 * p21 * m[2] + p20 * p22 * m[3] + p21 * p22 * m[4])
    )
    w0 = a0 + a1 * p10 + a2 * p20
    w1 = a1 * p11 + a2 * p21
    w2 = a2 * p22

    def combine(z, lo, hi, last):
        a = [
            w0 * b[k, z + 2, 8 + lo : 8 + hi] + w1 * v1[k, z + 1, 8 + lo : 8 + hi] + w2 * last(k)
            for k in range(3)
        ]
        g = [grad[k, z + 1, lo:hi] for k in range(3)]
        return a, g, g[0] * a[0] + g[1] * a[1] + g[2] * a[2]

    for side, z in ((0, -1), (1, Z)):
        a, g, along = combine(z, 0, Y, lambda k: v2_far[k, side])
        c0[z + 1] = -a[0] * (g[0] * late[side, 1] + late[side, 0]) - late[side, 1] * along

    copies = []

    def send(n, source, target):
        copies.append(pltpu.make_async_copy(source, target, sems.at[n]))
        copies[-1].start()

    def coupling(z):
        a, g, along = combine(z, 0, Y, lambda k: v2[k, z + 1, 8 : 8 + Y])
        fl = [f[k, z] for k in range(3)]
        rest = g[0] * fl[0] + g[1] * fl[1] + g[2] * fl[2] + temporal[z]
        for k in range(3):
            adj[k, z] = a[k]
        send(z, adj.at[:, z], adj_out.at[:, z])
        c0[z + 1] = -a[0] * rest - fl[0] * along
        c1[z, 8 : 8 + Y] = -a[1] * rest - fl[1] * along
        c2[z] = -a[2] * rest - fl[2] * along
        out0[z] = along
        a, g, along = combine(z, Y, R, lambda k: v2[k, z + 1, 8 + Y : 8 + R])
        rows = [late_rows[k, z] for k in range(4)]
        rest = g[0] * rows[1] + g[1] * rows[2] + g[2] * rows[3] + rows[0]
        side = -a[1] * rest - rows[2] * along
        c1[z, 0:8] = side
        c1[z, 8 + Y : 16 + Y] = side

    def spread(z):
        left, right = lane_sides(c2[z])
        total = (c0[z + 2] - c0[z]) + (c1[z, 9 : 9 + Y] - c1[z, 7 : 7 + Y]) + (right - left)
        half = total * -0.25
        along = out0[z]
        out0[z] = half + along
        out1[z] = half - along
        send(Z + z, out0.at[z], out0_out.at[z])
        send(2 * Z + z, out1.at[z], out1_out.at[z])

    coupling(0)
    for z in range(1, Z):
        coupling(z)
        spread(z - 1)
    spread(Z - 1)
    for copy in copies:
        copy.wait()


def vmem(*dims):
    return pltpu.VMEM(dims, F32)


def pinned(array):
    return pltpu.with_memory_space_constraint(array, pltpu.VMEM)


def hbm(*arrays):
    return [pltpu.with_memory_space_constraint(array, pltpu.HBM) for array in arrays]


def shape(*dims):
    return jax.ShapeDtypeStruct(dims, F32)


def shards(image0, image1, flow, cotangent):
    nz, ny = lax.axis_size("gz"), lax.axis_size("gy")
    devices = nz * ny

    side, middle = pl.pallas_call(
        pack_rows,
        in_specs=[HB] * 4,
        out_specs=[VM] * 2,
        out_shape=[vmem(2, Z, 8, X)] * 2,
        scratch_shapes=[
            pltpu.VMEM((2, Z, 8, X), F32),
            pltpu.VMEM((2, Z, 8, X), F32),
            pltpu.VMEM((2, 3, Z, 8, X), F32),
            pltpu.VMEM((2, 3, Z, 8, X), F32),
            pltpu.SemaphoreType.DMA((2, 4)),
        ],
        compiler_params=params(8),
        name="pack_rows",
    )(*hbm(image0, image1, cotangent, flow))

    def swaps(count, start):
        pairs = [(i, i + 1) for i in range(start, count - 1, 2)]
        return pairs + [(j, i) for i, j in pairs]

    own_side = side
    middle = lax.ppermute(middle, "gy", swaps(ny, 1))
    side = lax.ppermute(side, "gy", swaps(ny, 0))

    fields = [vmem(1, Z + 4, PAD, X), vmem(3, Z + 4, PAD, X), vmem(3, Z + 2, PAD, X), vmem(3, Z + 2, R, X)]
    mean, b, temporal, flow = pl.pallas_call(
        load,
        in_specs=[HB] * 5,
        out_specs=[VM] * 4,
        out_shape=fields[:2] + [vmem(Z, Y, X), vmem(3, Z, Y, X)],
        scratch_shapes=[
            pltpu.VMEM((Z, Y, X), F32),
            pltpu.VMEM((Z, Y, X), F32),
            pltpu.SemaphoreType.DMA((4,)),
        ],
        compiler_params=params(12),
        name="load",
    )(*hbm(image0, image1, cotangent, flow), own_side)

    ring, late_rows, inner, outer = pl.pallas_call(
        pack_slabs,
        in_specs=[VM] * 4,
        out_specs=[VM] * 4,
        out_shape=[vmem(4, Z, 8, X)] * 2 + [vmem(8, R, X)] * 2,
        compiler_params=params(8),
        name="pack_slabs",
    )(mean, b, pinned(middle), pinned(side))
    outer = lax.ppermute(outer, "gz", swaps(nz, 1))
    inner = lax.ppermute(inner, "gz", swaps(nz, 0))

    *fields_own, own_sums, inner_far, outer_far = pl.pallas_call(
        krylov_own,
        in_specs=[VM] * 5,
        out_specs=[VM] * 7,
        out_shape=fields + [vmem(3, 8, X), vmem(5, Y, X), vmem(5, Y, X)],
        compiler_params=params(12),
        input_output_aliases={0: 0, 1: 1},
        name="krylov_own",
    )(mean, b, temporal, flow, ring)
    outer_far = lax.ppermute(outer_far, "gz", swaps(nz, 1))
    inner_far = lax.ppermute(inner_far, "gz", swaps(nz, 0))

    _, b, v1, grad, v2, near_sums = pl.pallas_call(
        krylov_near,
        in_specs=[VM] * 7,
        out_specs=[VM] * 6,
        out_shape=fields + [vmem(3, Z + 2, PAD, X), vmem(6, 8, X)],
        input_output_aliases={2 + n: n for n in range(4)},
        compiler_params=params(12),
        name="krylov_near",
    )(pinned(outer), pinned(inner), *fields_own, own_sums)

    v2_far, late, sums = pl.pallas_call(
        krylov_far,
        in_specs=[VM] * 6,
        out_specs=[VM] * 3,
        out_shape=[vmem(3, 2, Y, X), vmem(2, 2, Y, X), vmem(devices, 128)],
        compiler_params=params(12),
        name="krylov_far",
    )(pinned(outer_far), pinned(inner_far), v1, v2, grad, near_sums)

    sums = lax.all_to_all(sums.reshape(devices, 1, 128), ("gz", "gy"), 0, 0).reshape(devices, 128)

    return pl.pallas_call(
        finish,
        in_specs=[VM] * 10,
        out_specs=[HB] * 3,
        out_shape=[shape(3, Z, Y, X), shape(Z, Y, X), shape(Z, Y, X)],
        scratch_shapes=[
            pltpu.VMEM((3, Z, Y, X), F32),
            pltpu.VMEM((Z, Y, X), F32),
            pltpu.VMEM((Z, Y, X), F32),
            pltpu.VMEM((Z + 2, Y, X), F32),
            pltpu.VMEM((Z, Y + 16, X), F32),
            pltpu.VMEM((Z, Y, X), F32),
            pltpu.SemaphoreType.DMA((3 * Z,)),
        ],
        compiler_params=params(12),
        name="finish",
    )(sums, b, v1, v2, v2_far, grad, temporal, flow, late_rows, late)


def solution(mesh):
    return jax.shard_map(
        shards,
        mesh=mesh,
        in_specs=(
            P("gz", "gy", None),
            P("gz", "gy", None),
            P(None, "gz", "gy", None),
            P(None, "gz", "gy", None),
        ),
        out_specs=(P(None, "gz", "gy", None), P("gz", "gy", None), P("gz", "gy", None)),
        check_vma=False,
    )
```

```python
import functools

import jax
import jax.numpy as jnp
from jax import lax
from jax.experimental import pallas as pl
from jax.experimental.pallas import tpu as pltpu
from jax.sharding import PartitionSpec as P

Z, Y, X = 4, 64, 256
H = X // 2
R = Y + 8
PAD = R + 16
F32 = jnp.float32
VM = pl.BlockSpec(memory_space=pltpu.VMEM)
HB = pl.BlockSpec(memory_space=pltpu.HBM)


def params(mib):
    return pltpu.CompilerParams(vmem_limit_bytes=mib * 1024 * 1024)


def lane_sides(v):
    lane = lax.broadcasted_iota(jnp.int32, v.shape[:-1] + (H,), v.ndim - 1)
    first, last = lane == 0, lane == H - 1
    a, b = v[..., :H], v[..., H:]
    ra, rb = pltpu.roll(a, 1, v.ndim - 1), pltpu.roll(b, 1, v.ndim - 1)
    qa, qb = pltpu.roll(a, H - 1, v.ndim - 1), pltpu.roll(b, H - 1, v.ndim - 1)
    left = jnp.concatenate([jnp.where(first, 0.0, ra), jnp.where(first, ra, rb)], axis=-1)
    right = jnp.concatenate([jnp.where(last, qb, qa), jnp.where(last, 0.0, qb)], axis=-1)
    return left, right


def pack_rows(i0, i1, c, f, side, middle, t0, t1, tc, tf, sems):
    copies = []
    for s, lo in enumerate((0, Y - 8)):
        rows = pl.ds(lo, 8)
        for n, (src, dst) in enumerate(((i0, t0), (i1, t1))):
            copies.append(pltpu.make_async_copy(src.at[:, rows], dst.at[s], sems.at[s, n]))
        for n, (src, dst) in enumerate(((c, tc), (f, tf))):
            copies.append(pltpu.make_async_copy(src.at[:, :, rows], dst.at[s], sems.at[s, n + 2]))
    for copy in copies:
        copy.start()
    for copy in copies:
        copy.wait()
    odd = lax.rem(lax.axis_index("gy"), 2) == 1
    sub = lax.broadcasted_iota(jnp.int32, (8, X), 0)

    def roll(v, n):
        return pltpu.roll(v, n, 0)

    for z in range(Z):
        messages = []
        for s in range(2):
            fields = [(t0[s, z] + t1[s, z]) * 0.5] + [tc[s, k, z] for k in range(3)]
            late = [t1[s, z] - t0[s, z]] + [tf[s, k, z] for k in range(3)]
            for p in range(2):
                one, two, one_late, two_late = fields[2 * p], fields[2 * p + 1], late[2 * p], late[2 * p + 1]
                if s == 0:
                    low, high, third, fourth = one, roll(two, 5), roll(one_late, 3), roll(two_late, 4)
                else:
                    low, high, third, fourth = roll(two, 3), one, roll(one_late, 4), roll(two_late, 5)
                messages.append(
                    jnp.where(sub < 3, low, jnp.where(sub == 3, third, jnp.where(sub == 4, fourth, high)))
                )
        for p in range(2):
            down, up = messages[p], messages[2 + p]
            side[p, z] = jnp.where(odd, down, up)
            middle[p, z] = jnp.where(odd, up, down)


def load(i0, i1, c, f, after, mean, b, temporal, flow, t0, t1, sems):
    del after
    copies = [
        pltpu.make_async_copy(i0, t0, sems.at[0]),
        pltpu.make_async_copy(i1, t1, sems.at[1]),
        pltpu.make_async_copy(c, b.at[:, 2 : 2 + Z, 8 : 8 + Y], sems.at[2]),
        pltpu.make_async_copy(f, flow, sems.at[3]),
    ]
    for copy in copies:
        copy.start()
    for copy in copies[:2]:
        copy.wait()
    for z in range(Z):
        put(mean, 0, z + 2, 0, (t0[z] + t1[z]) * 0.5)
        temporal[z] = t1[z] - t0[z]
    copies[2].wait()
    for z in range(Z):
        for k in range(3):
            b[k, z + 2, 8 + R : PAD] = b[k, z + 2, 8:16]
    copies[3].wait()


def pack_slabs(mean, b, middle, side, ring, late_rows, inner, outer):
    is_one = lax.rem(lax.axis_index("gz"), 2)
    odd = lax.rem(lax.axis_index("gy"), 2) == 1
    sub = lax.broadcasted_iota(jnp.int32, (8, X), 0)

    def roll(v, n):
        return pltpu.roll(v, n, 0)

    for z in range(Z):
        for p in range(2):
            a = jnp.where(odd, middle[p, z], side[p, z])
            b_tile = jnp.where(odd, side[p, z], middle[p, z])
            ring[2 * p, z] = jnp.where(sub < 3, a, jnp.where(sub >= 5, b_tile, 0.0))
            ring[2 * p + 1, z] = jnp.where(sub < 3, roll(a, 3), jnp.where(sub >= 5, roll(b_tile, 5), 0.0))
            late_rows[2 * p, z] = jnp.where(sub == 0, roll(a, 5), roll(b_tile, 4))
            late_rows[2 * p + 1, z] = jnp.where(sub == 0, roll(a, 4), roll(b_tile, 3))
    for near, first, step in (
        (inner, (Z - 1) * (1 - is_one), 2 * is_one - 1),
        (outer, (Z - 1) * is_one, 1 - 2 * is_one),
    ):
        for k in range(4):
            source, n = (b, k - 1) if k else (mean, 0)
            near[k, 0:Y] = source[n, first + 2, 8 : 8 + Y]
            near[k, Y : 2 * Y] = source[n, first + step + 2, 8 : 8 + Y]
            one, two = ring[k, first], ring[k, first + step]
            tile = jnp.where(sub == 2, roll(two, 2), jnp.where(sub == 5, roll(two, 6), one))
            near[k, 2 * Y : 2 * Y + 8] = tile


class Stencil:
    def __init__(self):
        self.gz, gy = lax.axis_index("gz"), lax.axis_index("gy")
        self.nz, ny = lax.axis_size("gz"), lax.axis_size("gy")
        row = lax.broadcasted_iota(jnp.int32, (24, X), 0) + (R - 24)
        after = jnp.where(gy < ny - 1, 1.0, 0.0)
        before = jnp.where(gy > 0, 1.0, 0.0)
        self.keep = jnp.where(row < Y, 1.0, jnp.where(row < Y + 4, after, before))

    def inside(self, z):
        slab = self.gz * Z + z
        return jnp.where((slab >= 0) & (slab < self.nz * Z), 1.0, 0.0)

    def mask(self, value, z, r):
        value = value * self.inside(z)
        return value * self.keep if r == R - 24 else value


def tiles(value, rows):
    total = value[0:8]
    for r in range(8, rows, 8):
        total = total + value[r : r + 8]
    return total


def put(ref, k, z, r, value):
    rows = value.shape[0]
    ref[k, z, 8 + r : 8 + r + rows] = value
    if r == 0:
        ref[k, z, 8 + R : PAD] = value[0:8]
    if r + rows == R:
        ref[k, z, 0:8] = value[rows - 8 : rows]


def row_sides(ref, k, z, r, rows=24):
    return ref[k, z, 7 + r : 7 + r + rows], ref[k, z, 9 + r : 9 + r + rows]


def apply(g, vs, sums):
    dot = g[0] * vs[0] + g[1] * vs[1] + g[2] * vs[2]
    return [g[k] * dot + (3.0 * vs[k] - 0.5 * sums[k]) for k in range(3)]


def flat(ref, k, z, r, rows=24):
    v = ref[k, z, 8 + r : 8 + r + rows]
    left, right = lane_sides(v)
    before, after = row_sides(ref, k, z, r, rows)
    return v, (before + after) + (left + right)


def first_step(st, mean, b, v1, grad, z, r, parts):
    at = z + 2
    rows = 24 if r < R - 24 else 16
    mid = slice(8 + r, 32 + r)
    left, right = lane_sides(mean[0, at, mid])
    before, after = row_sides(mean, 0, at, r)
    g = [(mean[0, at + 1, mid] - mean[0, at - 1, mid]) * 0.5, (after - before) * 0.5, (right - left) * 0.5]
    vs, totals = [], []
    for k in range(3):
        grad[k, z + 1, r : r + 24] = g[k]
        v, total = flat(b, k, at, r)
        vs.append(v)
        totals.append(total + (b[k, at - 1, mid] + b[k, at + 1, mid]))
    parts = list(parts)
    for k, image in enumerate(apply(g, vs, totals)):
        out = st.mask(image, z, r)
        put(v1, k, z + 1, r, out)
        for n, product in enumerate((vs[k] * vs[k], vs[k] * out, out * out)):
            parts[n] = parts[n] + tiles(product, rows)
    return parts


def krylov_own(mean_in, b_in, temporal, f, ring, mean, b, v1, grad, sums, inner_far, outer_far):
    del mean_in, b_in
    st = Stencil()
    is_one = lax.rem(st.gz, 2)
    for z in range(Z):
        put(mean, 0, z + 2, Y, ring[0, z])
        for k in range(3):
            put(b, k, z + 2, Y, ring[k + 1, z])

    def slab(j, parts):
        for r in range(0, R, 24):
            parts = first_step(st, mean, b, v1, grad, j + 1, r, parts)
        return tuple(parts)

    parts = lax.fori_loop(0, Z - 2, slab, (jnp.zeros((8, X), F32),) * 3)
    for n in range(3):
        sums[n] = parts[n]
    for far, first, second in (
        (inner_far, (Z - 1) * (1 - is_one), Z - 2 + is_one * (3 - Z)),
        (outer_far, (Z - 1) * is_one, 1 + is_one * (Z - 3)),
    ):
        for k in range(3):
            far[k] = v1[k, second + 1, 8 : 8 + Y]
        left, right = lane_sides(mean[0, first + 2, 8 : 8 + Y])
        before, after = row_sides(mean, 0, first + 2, 0, Y)
        far[3] = ((after - before) * f[1, first] + (right - left) * f[2, first]) * 0.5 + temporal[first]
        far[4] = f[0, first]


def krylov_near(outer, inner, mean_in, b_in, v1_in, grad_in, own_sums, mean, b, v1, grad, v2, sums):
    del mean_in, b_in, v1_in, grad_in
    sub = lax.broadcasted_iota(jnp.int32, (8, X), 0)
    st = Stencil()
    is_one = lax.rem(st.gz, 2)
    for near, upper in ((inner, 1 - is_one), (outer, is_one)):
        at_one, at_two = jnp.where(upper == 1, Z + 2, 1), jnp.where(upper == 1, Z + 3, 0)
        for k in range(4):
            target, n = (b, k - 1) if k else (mean, 0)
            tile = near[k, 2 * Y : 2 * Y + 8]
            put(target, n, at_one, 0, near[k, 0:Y])
            put(target, n, at_one, Y, tile)
            put(target, n, at_two, 0, near[k, Y : 2 * Y])
            put(target, n, at_two, Y, jnp.where(sub == 0, pltpu.roll(tile, 6, 0), pltpu.roll(tile, 2, 0)))

    zero = jnp.zeros((8, X), F32)

    def first(j, carry):
        z = jnp.where(j < 2, j - 1, j + Z - 3)
        mine = jnp.where((z >= 0) & (z < Z), 1.0, 0.0)
        parts = [zero] * 3
        for r in range(0, R, 24):
            parts = first_step(st, mean, b, v1, grad, z, r, parts)
        return tuple(m + mine * t for m, t in zip(carry, parts))

    m0, m1, m2 = lax.fori_loop(0, 4, first, tuple(own_sums[n] for n in range(3)), unroll=True)

    def second(z, carry):
        m3, m4 = carry
        for r in range(0, R, 24):
            rows = 24 if r < R - 24 else 16
            g = [grad[k, z + 1, r : r + 24] for k in range(3)]
            vs, totals = [], []
            for k in range(3):
                v, total = flat(v1, k, z + 1, r)
                vs.append(v)
                totals.append(total + (v1[k, z, 8 + r : 32 + r] + v1[k, z + 2, 8 + r : 32 + r]))
            for k, image in enumerate(apply(g, vs, totals)):
                out = st.mask(image, z, r)
                put(v2, k, z + 1, r, out)
                m3 = m3 + tiles(vs[k] * out, rows)
                m4 = m4 + tiles(out * out, rows)
        return m3, m4

    m3, m4 = lax.fori_loop(0, Z, second, (zero,) * 2, unroll=True)

    def third(z, m5):
        low = jnp.where(z > 0, 1.0, 0.0)
        for r in range(0, R, 24):
            rows = 24 if r < R - 24 else 16
            dot = 0.0
            for k in range(3):
                v, total = flat(v2, k, z + 1, r)
                dot = dot + grad[k, z + 1, r : r + 24] * v
                below = v2[k, jnp.maximum(z, 1), 8 + r : 32 + r] * low
                m5 = m5 + tiles(v * (3.0 * v - 0.5 * total - below), rows)
            m5 = m5 + tiles(dot * dot, rows)
        return m5

    m5 = lax.fori_loop(0, Z, third, zero, unroll=True)
    for n, m in enumerate((m0, m1, m2, m3, m4, m5)):
        sums[n] = m


def krylov_far(outer_far, inner_far, v1, v2, grad, near_sums, v2_far, late, sums):
    st = Stencil()
    is_one = lax.rem(st.gz, 2)

    def face(far, side, cross):
        z = jnp.where(side == 1, Z, -1)
        edge = jnp.where(side == 1, Z, 1)
        scale = st.inside(z)
        for k in range(2):
            late[side, k] = far[3 + k]
        for r in range(0, Y, 16):
            g = [grad[k, z + 1, r : r + 16] for k in range(3)]
            vs, totals = [], []
            for k in range(3):
                v, total = flat(v1, k, z + 1, r, 16)
                vs.append(v)
                totals.append(total + (far[k, r : r + 16] + v1[k, edge, 8 + r : 24 + r]))
            for k, image in enumerate(apply(g, vs, totals)):
                out = image * scale
                v2_far[k, side, r : r + 16] = out
                cross = cross + tiles(v2[k, edge, 8 + r : 24 + r] * out, 16)
        return cross

    cross = face(inner_far, 1 - is_one, jnp.zeros((8, X), F32))
    cross = face(outer_far, is_one, cross)
    lane = lax.broadcasted_iota(jnp.int32, sums.shape, 1)
    out = jnp.zeros(sums.shape, F32)
    for n in range(6):
        m = near_sums[n] - 0.5 * cross if n == 5 else near_sums[n]
        out = jnp.where(lane == n, jnp.sum(m), out)
    sums[...] = out


def finish(
    sums, b, v1, v2, v2_far, grad, temporal, f, late_rows, late, adj_out, out0_out, out1_out,
    adj, out0, out1, c0, c1, c2, sems,
):
    total = jnp.sum(sums[...], axis=0, keepdims=True)
    lane = lax.broadcasted_iota(jnp.int32, total.shape, 1)
    m = [jnp.sum(jnp.where(lane == k, total, 0.0), axis=1, keepdims=True) for k in range(6)]
    a0 = m[0] / m[1]
    least, mean_eigenvalue = 1e-12 * m[0], m[1] / m[0]
    rr1 = jnp.maximum(m[0] - 2.0 * a0 * m[1] + a0 * a0 * m[2], least)
    b0 = rr1 / m[0]
    p10, p11 = 1.0 + b0, -a0
    curve1 = p10 * p10 * m[1] + 2.0 * p10 * p11 * m[2] + p11 * p11 * m[3]
    a1 = rr1 / jnp.maximum(curve1, 1e-6 * rr1 * mean_eigenvalue)
    r21, r22 = -a0 - a1 * p10, -a1 * p11
    rr2 = m[0] + r21 * r21 * m[2] + r22 * r22 * m[4] + 2.0 * (r21 * m[1] + r22 * m[2] + r21 * r22 * m[3])
    rr2 = jnp.maximum(rr2, least)
    b1 = rr2 / rr1
    p20, p21, p22 = 1.0 + b1 * p10, r21 + b1 * p11, r22
    curve2 = p20 * p20 * m[1] + p21 * p21 * m[3] + p22 * p22 * m[5]
    curve2 = curve2 + 2.0 * (p20 * p21 * m[2] + p20 * p22 * m[3] + p21 * p22 * m[4])
    a2 = rr2 / jnp.maximum(curve2, 1e-6 * rr2 * mean_eigenvalue)
    w0 = a0 + a1 * p10 + a2 * p20
    w1 = a1 * p11 + a2 * p21
    w2 = a2 * p22

    def combine(z, lo, hi, last):
        a = [
            w0 * b[k, z + 2, 8 + lo : 8 + hi] + w1 * v1[k, z + 1, 8 + lo : 8 + hi] + w2 * last(k)
            for k in range(3)
        ]
        g = [grad[k, z + 1, lo:hi] for k in range(3)]
        return a, g, g[0] * a[0] + g[1] * a[1] + g[2] * a[2]

    for side, z in ((0, -1), (1, Z)):
        a, g, along = combine(z, 0, Y, lambda k: v2_far[k, side])
        c0[z + 1] = -a[0] * (g[0] * late[side, 1] + late[side, 0]) - late[side, 1] * along

    copies = []

    def send(n, source, target):
        copies.append(pltpu.make_async_copy(source, target, sems.at[n]))
        copies[-1].start()

    def coupling(z):
        a, g, along = combine(z, 0, Y, lambda k: v2[k, z + 1, 8 : 8 + Y])
        fl = [f[k, z] for k in range(3)]
        rest = g[0] * fl[0] + g[1] * fl[1] + g[2] * fl[2] + temporal[z]
        for k in range(3):
            adj[k, z] = a[k]
        send(z, adj.at[:, z], adj_out.at[:, z])
        c0[z + 1] = -a[0] * rest - fl[0] * along
        c1[z, 8 : 8 + Y] = -a[1] * rest - fl[1] * along
        c2[z] = -a[2] * rest - fl[2] * along
        out0[z] = along
        a, g, along = combine(z, Y, R, lambda k: v2[k, z + 1, 8 + Y : 8 + R])
        rows = [late_rows[k, z] for k in range(4)]
        rest = g[0] * rows[1] + g[1] * rows[2] + g[2] * rows[3] + rows[0]
        side = -a[1] * rest - rows[2] * along
        c1[z, 0:8] = side
        c1[z, 8 + Y : 16 + Y] = side

    def spread(z):
        left, right = lane_sides(c2[z])
        total = (c0[z + 2] - c0[z]) + (c1[z, 9 : 9 + Y] - c1[z, 7 : 7 + Y]) + (right - left)
        half = total * -0.25
        along = out0[z]
        out0[z] = half + along
        out1[z] = half - along
        send(Z + z, out0.at[z], out0_out.at[z])
        send(2 * Z + z, out1.at[z], out1_out.at[z])

    coupling(0)
    for z in range(1, Z):
        coupling(z)
        spread(z - 1)
    spread(Z - 1)
    for copy in copies:
        copy.wait()


def vmem(*dims):
    return pltpu.VMEM(dims, F32)


def pinned(array):
    return pltpu.with_memory_space_constraint(array, pltpu.VMEM)


def hbm(*arrays):
    return [pltpu.with_memory_space_constraint(array, pltpu.HBM) for array in arrays]


def shape(*dims):
    return jax.ShapeDtypeStruct(dims, F32)


def shards(image0, image1, flow, cotangent):
    nz, ny = lax.axis_size("gz"), lax.axis_size("gy")
    devices = nz * ny

    side, middle = pl.pallas_call(
        pack_rows,
        in_specs=[HB] * 4,
        out_specs=[VM] * 2,
        out_shape=[vmem(2, Z, 8, X)] * 2,
        scratch_shapes=[
            pltpu.VMEM((2, Z, 8, X), F32),
            pltpu.VMEM((2, Z, 8, X), F32),
            pltpu.VMEM((2, 3, Z, 8, X), F32),
            pltpu.VMEM((2, 3, Z, 8, X), F32),
            pltpu.SemaphoreType.DMA((2, 4)),
        ],
        compiler_params=params(8),
        name="pack_rows",
    )(*hbm(image0, image1, cotangent, flow))

    def swaps(count, start):
        pairs = [(i, i + 1) for i in range(start, count - 1, 2)]
        return pairs + [(j, i) for i, j in pairs]

    own_side = side
    middle = lax.ppermute(middle, "gy", swaps(ny, 1))
    side = lax.ppermute(side, "gy", swaps(ny, 0))

    fields = [vmem(1, Z + 4, PAD, X), vmem(3, Z + 4, PAD, X), vmem(3, Z + 2, PAD, X), vmem(3, Z + 2, R, X)]
    mean, b, temporal, flow = pl.pallas_call(
        load,
        in_specs=[HB] * 5,
        out_specs=[VM] * 4,
        out_shape=fields[:2] + [vmem(Z, Y, X), vmem(3, Z, Y, X)],
        scratch_shapes=[
            pltpu.VMEM((Z, Y, X), F32),
            pltpu.VMEM((Z, Y, X), F32),
            pltpu.SemaphoreType.DMA((4,)),
        ],
        compiler_params=params(12),
        name="load",
    )(*hbm(image0, image1, cotangent, flow), own_side)

    ring, late_rows, inner, outer = pl.pallas_call(
        pack_slabs,
        in_specs=[VM] * 4,
        out_specs=[VM] * 4,
        out_shape=[vmem(4, Z, 8, X)] * 2 + [vmem(4, 2 * Y + 8, X)] * 2,
        compiler_params=params(8),
        name="pack_slabs",
    )(mean, b, pinned(middle), pinned(side))
    outer = lax.ppermute(outer, "gz", swaps(nz, 1))
    inner = lax.ppermute(inner, "gz", swaps(nz, 0))

    *fields_own, own_sums, inner_far, outer_far = pl.pallas_call(
        krylov_own,
        in_specs=[VM] * 5,
        out_specs=[VM] * 7,
        out_shape=fields + [vmem(3, 8, X), vmem(5, Y, X), vmem(5, Y, X)],
        compiler_params=params(12),
        input_output_aliases={0: 0, 1: 1},
        name="krylov_own",
    )(mean, b, temporal, flow, ring)
    outer_far = lax.ppermute(outer_far, "gz", swaps(nz, 1))
    inner_far = lax.ppermute(inner_far, "gz", swaps(nz, 0))

    _, b, v1, grad, v2, near_sums = pl.pallas_call(
        krylov_near,
        in_specs=[VM] * 7,
        out_specs=[VM] * 6,
        out_shape=fields + [vmem(3, Z + 2, PAD, X), vmem(6, 8, X)],
        input_output_aliases={2 + n: n for n in range(4)},
        compiler_params=params(12),
        name="krylov_near",
    )(pinned(outer), pinned(inner), *fields_own, own_sums)

    v2_far, late, sums = pl.pallas_call(
        krylov_far,
        in_specs=[VM] * 6,
        out_specs=[VM] * 3,
        out_shape=[vmem(3, 2, Y, X), vmem(2, 2, Y, X), vmem(devices, 128)],
        compiler_params=params(12),
        name="krylov_far",
    )(pinned(outer_far), pinned(inner_far), v1, v2, grad, near_sums)

    sums = lax.all_to_all(sums.reshape(devices, 1, 128), ("gz", "gy"), 0, 0).reshape(devices, 128)

    return pl.pallas_call(
        finish,
        in_specs=[VM] * 10,
        out_specs=[HB] * 3,
        out_shape=[shape(3, Z, Y, X), shape(Z, Y, X), shape(Z, Y, X)],
        scratch_shapes=[
            pltpu.VMEM((3, Z, Y, X), F32),
            pltpu.VMEM((Z, Y, X), F32),
            pltpu.VMEM((Z, Y, X), F32),
            pltpu.VMEM((Z + 2, Y, X), F32),
            pltpu.VMEM((Z, Y + 16, X), F32),
            pltpu.VMEM((Z, Y, X), F32),
            pltpu.SemaphoreType.DMA((3 * Z,)),
        ],
        compiler_params=params(12),
        name="finish",
    )(sums, b, v1, v2, v2_far, grad, temporal, flow, late_rows, late)


def solution(mesh):
    return jax.shard_map(
        shards,
        mesh=mesh,
        in_specs=(
            P("gz", "gy", None),
            P("gz", "gy", None),
            P(None, "gz", "gy", None),
            P(None, "gz", "gy", None),
        ),
        out_specs=(P(None, "gz", "gy", None), P("gz", "gy", None), P("gz", "gy", None)),
        check_vma=False,
    )
```

```python
import functools

import jax
import jax.numpy as jnp
from jax import lax
from jax.experimental import pallas as pl
from jax.experimental.pallas import tpu as pltpu
from jax.sharding import PartitionSpec as P

Z, Y, X = 4, 64, 256
H = X // 2
R = Y + 8
PAD = R + 16
F32 = jnp.float32
VM = pl.BlockSpec(memory_space=pltpu.VMEM)
HB = pl.BlockSpec(memory_space=pltpu.HBM)


def params(mib):
    return pltpu.CompilerParams(vmem_limit_bytes=mib * 1024 * 1024)


def lane_sides(v):
    lane = lax.broadcasted_iota(jnp.int32, v.shape[:-1] + (H,), v.ndim - 1)
    first, last = lane == 0, lane == H - 1
    a, b = v[..., :H], v[..., H:]
    ra, rb = pltpu.roll(a, 1, v.ndim - 1), pltpu.roll(b, 1, v.ndim - 1)
    qa, qb = pltpu.roll(a, H - 1, v.ndim - 1), pltpu.roll(b, H - 1, v.ndim - 1)
    left = jnp.concatenate([jnp.where(first, 0.0, ra), jnp.where(first, ra, rb)], axis=-1)
    right = jnp.concatenate([jnp.where(last, qb, qa), jnp.where(last, 0.0, qb)], axis=-1)
    return left, right


def pack_rows(i0, i1, c, f, side, middle, t0, t1, tc, tf, sems):
    copies = []
    for s, lo in enumerate((0, Y - 8)):
        rows = pl.ds(lo, 8)
        for n, (src, dst) in enumerate(((i0, t0), (i1, t1))):
            copies.append(pltpu.make_async_copy(src.at[:, rows], dst.at[s], sems.at[s, n]))
        for n, (src, dst) in enumerate(((c, tc), (f, tf))):
            copies.append(pltpu.make_async_copy(src.at[:, :, rows], dst.at[s], sems.at[s, n + 2]))
    for copy in copies:
        copy.start()
    for copy in copies:
        copy.wait()
    odd = lax.rem(lax.axis_index("gy"), 2) == 1
    sub = lax.broadcasted_iota(jnp.int32, (8, X), 0)

    def roll(v, n):
        return pltpu.roll(v, n, 0)

    for z in range(Z):
        messages = []
        for s in range(2):
            fields = [(t0[s, z] + t1[s, z]) * 0.5] + [tc[s, k, z] for k in range(3)]
            late = [t1[s, z] - t0[s, z]] + [tf[s, k, z] for k in range(3)]
            for p in range(2):
                one, two, one_late, two_late = fields[2 * p], fields[2 * p + 1], late[2 * p], late[2 * p + 1]
                if s == 0:
                    low, high, third, fourth = one, roll(two, 5), roll(one_late, 3), roll(two_late, 4)
                else:
                    low, high, third, fourth = roll(two, 3), one, roll(one_late, 4), roll(two_late, 5)
                messages.append(
                    jnp.where(sub < 3, low, jnp.where(sub == 3, third, jnp.where(sub == 4, fourth, high)))
                )
        for p in range(2):
            down, up = messages[p], messages[2 + p]
            side[p, z] = jnp.where(odd, down, up)
            middle[p, z] = jnp.where(odd, up, down)


def load(i0, i1, c, f, after, mean, b, temporal, flow, t0, t1, sems):
    del after
    copies = [
        pltpu.make_async_copy(i0, t0, sems.at[0]),
        pltpu.make_async_copy(i1, t1, sems.at[1]),
        pltpu.make_async_copy(c, b.at[:, 2 : 2 + Z, 8 : 8 + Y], sems.at[2]),
        pltpu.make_async_copy(f, flow, sems.at[3]),
    ]
    for copy in copies:
        copy.start()
    for copy in copies[:2]:
        copy.wait()
    for z in range(Z):
        put(mean, 0, z + 2, 0, (t0[z] + t1[z]) * 0.5)
        temporal[z] = t1[z] - t0[z]
    copies[2].wait()
    for z in range(Z):
        for k in range(3):
            b[k, z + 2, 8 + R : PAD] = b[k, z + 2, 8:16]
    copies[3].wait()


def pack_slabs(mean, b, middle, side, ring, late_rows, inner, outer):
    is_one = lax.rem(lax.axis_index("gz"), 2)
    odd = lax.rem(lax.axis_index("gy"), 2) == 1
    sub = lax.broadcasted_iota(jnp.int32, (8, X), 0)

    def roll(v, n):
        return pltpu.roll(v, n, 0)

    for z in range(Z):
        for p in range(2):
            a = jnp.where(odd, middle[p, z], side[p, z])
            b_tile = jnp.where(odd, side[p, z], middle[p, z])
            ring[2 * p, z] = jnp.where(sub < 3, a, jnp.where(sub >= 5, b_tile, 0.0))
            ring[2 * p + 1, z] = jnp.where(sub < 3, roll(a, 3), jnp.where(sub >= 5, roll(b_tile, 5), 0.0))
            late_rows[2 * p, z] = jnp.where(sub == 0, roll(a, 5), roll(b_tile, 4))
            late_rows[2 * p + 1, z] = jnp.where(sub == 0, roll(a, 4), roll(b_tile, 3))
    for near, first, step in (
        (inner, (Z - 1) * (1 - is_one), 2 * is_one - 1),
        (outer, (Z - 1) * is_one, 1 - 2 * is_one),
    ):
        for k in range(4):
            source, n = (b, k - 1) if k else (mean, 0)
            near[k, 0:Y] = source[n, first + 2, 8 : 8 + Y]
            near[k, Y : 2 * Y] = source[n, first + step + 2, 8 : 8 + Y]
            one, two = ring[k, first], ring[k, first + step]
            tile = jnp.where(sub == 2, roll(two, 2), jnp.where(sub == 5, roll(two, 6), one))
            near[k, 2 * Y : 2 * Y + 8] = tile


class Stencil:
    def __init__(self):
        self.gz, gy = lax.axis_index("gz"), lax.axis_index("gy")
        self.nz, ny = lax.axis_size("gz"), lax.axis_size("gy")
        row = lax.broadcasted_iota(jnp.int32, (24, X), 0) + (R - 24)
        after = jnp.where(gy < ny - 1, 1.0, 0.0)
        before = jnp.where(gy > 0, 1.0, 0.0)
        self.keep = jnp.where(row < Y, 1.0, jnp.where(row < Y + 4, after, before))

    def inside(self, z):
        slab = self.gz * Z + z
        return jnp.where((slab >= 0) & (slab < self.nz * Z), 1.0, 0.0)

    def mask(self, value, z, r):
        value = value * self.inside(z)
        return value * self.keep if r == R - 24 else value


def tiles(value, rows):
    total = value[0:8]
    for r in range(8, rows, 8):
        total = total + value[r : r + 8]
    return total


def put(ref, k, z, r, value):
    rows = value.shape[0]
    ref[k, z, 8 + r : 8 + r + rows] = value
    if r == 0:
        ref[k, z, 8 + R : PAD] = value[0:8]
    if r + rows == R:
        ref[k, z, 0:8] = value[rows - 8 : rows]


def row_sides(ref, k, z, r, rows=24):
    return ref[k, z, 7 + r : 7 + r + rows], ref[k, z, 9 + r : 9 + r + rows]


def apply(g, vs, sums):
    dot = g[0] * vs[0] + g[1] * vs[1] + g[2] * vs[2]
    return [g[k] * dot + (3.0 * vs[k] - 0.5 * sums[k]) for k in range(3)]


def flat(ref, k, z, r, rows=24):
    v = ref[k, z, 8 + r : 8 + r + rows]
    left, right = lane_sides(v)
    before, after = row_sides(ref, k, z, r, rows)
    return v, (before + after) + (left + right)


def first_step(st, mean, b, v1, grad, z, r, parts):
    at = z + 2
    rows = 24 if r < R - 24 else 16
    mid = slice(8 + r, 32 + r)
    left, right = lane_sides(mean[0, at, mid])
    before, after = row_sides(mean, 0, at, r)
    g = [(mean[0, at + 1, mid] - mean[0, at - 1, mid]) * 0.5, (after - before) * 0.5, (right - left) * 0.5]
    vs, totals = [], []
    for k in range(3):
        grad[k, z + 1, r : r + 24] = g[k]
        v, total = flat(b, k, at, r)
        vs.append(v)
        totals.append(total + (b[k, at - 1, mid] + b[k, at + 1, mid]))
    parts = list(parts)
    for k, image in enumerate(apply(g, vs, totals)):
        out = st.mask(image, z, r)
        put(v1, k, z + 1, r, out)
        for n, product in enumerate((vs[k] * vs[k], vs[k] * out, out * out)):
            parts[n] = parts[n] + tiles(product, rows)
    return parts


def krylov_own(mean_in, b_in, temporal, f, ring, mean, b, v1, grad, sums, inner_far, outer_far):
    del mean_in, b_in
    st = Stencil()
    is_one = lax.rem(st.gz, 2)
    for z in range(Z):
        put(mean, 0, z + 2, Y, ring[0, z])
        for k in range(3):
            put(b, k, z + 2, Y, ring[k + 1, z])

    def slab(j, parts):
        for r in range(0, R, 24):
            parts = first_step(st, mean, b, v1, grad, j + 1, r, parts)
        return tuple(parts)

    parts = lax.fori_loop(0, Z - 2, slab, (jnp.zeros((8, X), F32),) * 3, unroll=True)
    for n in range(3):
        sums[n] = parts[n]
    for far, first, second in (
        (inner_far, (Z - 1) * (1 - is_one), Z - 2 + is_one * (3 - Z)),
        (outer_far, (Z - 1) * is_one, 1 + is_one * (Z - 3)),
    ):
        for k in range(3):
            far[k] = v1[k, second + 1, 8 : 8 + Y]
        left, right = lane_sides(mean[0, first + 2, 8 : 8 + Y])
        before, after = row_sides(mean, 0, first + 2, 0, Y)
        far[3] = ((after - before) * f[1, first] + (right - left) * f[2, first]) * 0.5 + temporal[first]
        far[4] = f[0, first]


def krylov_near(outer, inner, mean_in, b_in, v1_in, grad_in, own_sums, mean, b, v1, grad, v2, sums):
    del mean_in, b_in, v1_in, grad_in
    sub = lax.broadcasted_iota(jnp.int32, (8, X), 0)
    st = Stencil()
    is_one = lax.rem(st.gz, 2)
    for near, upper in ((inner, 1 - is_one), (outer, is_one)):
        at_one, at_two = jnp.where(upper == 1, Z + 2, 1), jnp.where(upper == 1, Z + 3, 0)
        for k in range(4):
            target, n = (b, k - 1) if k else (mean, 0)
            tile = near[k, 2 * Y : 2 * Y + 8]
            put(target, n, at_one, 0, near[k, 0:Y])
            put(target, n, at_one, Y, tile)
            put(target, n, at_two, 0, near[k, Y : 2 * Y])
            put(target, n, at_two, Y, jnp.where(sub == 0, pltpu.roll(tile, 6, 0), pltpu.roll(tile, 2, 0)))

    zero = jnp.zeros((8, X), F32)

    def first(j, carry):
        z = jnp.where(j < 2, j - 1, j + Z - 3)
        mine = jnp.where((z >= 0) & (z < Z), 1.0, 0.0)
        parts = [zero] * 3
        for r in range(0, R, 24):
            parts = first_step(st, mean, b, v1, grad, z, r, parts)
        return tuple(m + mine * t for m, t in zip(carry, parts))

    m0, m1, m2 = lax.fori_loop(0, 4, first, tuple(own_sums[n] for n in range(3)), unroll=True)

    def second(z, carry):
        m3, m4 = carry
        for r in range(0, R, 24):
            rows = 24 if r < R - 24 else 16
            g = [grad[k, z + 1, r : r + 24] for k in range(3)]
            vs, totals = [], []
            for k in range(3):
                v, total = flat(v1, k, z + 1, r)
                vs.append(v)
                totals.append(total + (v1[k, z, 8 + r : 32 + r] + v1[k, z + 2, 8 + r : 32 + r]))
            for k, image in enumerate(apply(g, vs, totals)):
                out = st.mask(image, z, r)
                put(v2, k, z + 1, r, out)
                m3 = m3 + tiles(vs[k] * out, rows)
                m4 = m4 + tiles(out * out, rows)
        return m3, m4

    m3, m4 = lax.fori_loop(0, Z, second, (zero,) * 2, unroll=True)

    def third(z, m5):
        low = jnp.where(z > 0, 1.0, 0.0)
        for r in range(0, R, 24):
            rows = 24 if r < R - 24 else 16
            dot = 0.0
            for k in range(3):
                v, total = flat(v2, k, z + 1, r)
                dot = dot + grad[k, z + 1, r : r + 24] * v
                below = v2[k, jnp.maximum(z, 1), 8 + r : 32 + r] * low
                m5 = m5 + tiles(v * (3.0 * v - 0.5 * total - below), rows)
            m5 = m5 + tiles(dot * dot, rows)
        return m5

    m5 = lax.fori_loop(0, Z, third, zero, unroll=True)
    for n, m in enumerate((m0, m1, m2, m3, m4, m5)):
        sums[n] = m


def krylov_far(outer_far, inner_far, v1, v2, grad, near_sums, v2_far, late, sums):
    st = Stencil()
    is_one = lax.rem(st.gz, 2)

    def face(far, side, cross):
        z = jnp.where(side == 1, Z, -1)
        edge = jnp.where(side == 1, Z, 1)
        scale = st.inside(z)
        for k in range(2):
            late[side, k] = far[3 + k]
        for r in range(0, Y, 16):
            g = [grad[k, z + 1, r : r + 16] for k in range(3)]
            vs, totals = [], []
            for k in range(3):
                v, total = flat(v1, k, z + 1, r, 16)
                vs.append(v)
                totals.append(total + (far[k, r : r + 16] + v1[k, edge, 8 + r : 24 + r]))
            for k, image in enumerate(apply(g, vs, totals)):
                out = image * scale
                v2_far[k, side, r : r + 16] = out
                cross = cross + tiles(v2[k, edge, 8 + r : 24 + r] * out, 16)
        return cross

    cross = face(inner_far, 1 - is_one, jnp.zeros((8, X), F32))
    cross = face(outer_far, is_one, cross)
    lane = lax.broadcasted_iota(jnp.int32, sums.shape, 1)
    out = jnp.zeros(sums.shape, F32)
    for n in range(6):
        m = near_sums[n] - 0.5 * cross if n == 5 else near_sums[n]
        out = jnp.where(lane == n, jnp.sum(m), out)
    sums[...] = out


def finish(
    sums, b, v1, v2, v2_far, grad, temporal, f, late_rows, late, adj_out, out0_out, out1_out,
    adj, out0, out1, c0, c1, c2, sems,
):
    total = jnp.sum(sums[...], axis=0, keepdims=True)
    lane = lax.broadcasted_iota(jnp.int32, total.shape, 1)
    m = [jnp.sum(jnp.where(lane == k, total, 0.0), axis=1, keepdims=True) for k in range(6)]
    a0 = m[0] / m[1]
    least, mean_eigenvalue = 1e-12 * m[0], m[1] / m[0]
    rr1 = jnp.maximum(m[0] - 2.0 * a0 * m[1] + a0 * a0 * m[2], least)
    b0 = rr1 / m[0]
    p10, p11 = 1.0 + b0, -a0
    curve1 = p10 * p10 * m[1] + 2.0 * p10 * p11 * m[2] + p11 * p11 * m[3]
    a1 = rr1 / jnp.maximum(curve1, 1e-6 * rr1 * mean_eigenvalue)
    r21, r22 = -a0 - a1 * p10, -a1 * p11
    rr2 = m[0] + r21 * r21 * m[2] + r22 * r22 * m[4] + 2.0 * (r21 * m[1] + r22 * m[2] + r21 * r22 * m[3])
    rr2 = jnp.maximum(rr2, least)
    b1 = rr2 / rr1
    p20, p21, p22 = 1.0 + b1 * p10, r21 + b1 * p11, r22
    curve2 = p20 * p20 * m[1] + p21 * p21 * m[3] + p22 * p22 * m[5]
    curve2 = curve2 + 2.0 * (p20 * p21 * m[2] + p20 * p22 * m[3] + p21 * p22 * m[4])
    a2 = rr2 / jnp.maximum(curve2, 1e-6 * rr2 * mean_eigenvalue)
    w0 = a0 + a1 * p10 + a2 * p20
    w1 = a1 * p11 + a2 * p21
    w2 = a2 * p22

    def combine(z, lo, hi, last):
        a = [
            w0 * b[k, z + 2, 8 + lo : 8 + hi] + w1 * v1[k, z + 1, 8 + lo : 8 + hi] + w2 * last(k)
            for k in range(3)
        ]
        g = [grad[k, z + 1, lo:hi] for k in range(3)]
        return a, g, g[0] * a[0] + g[1] * a[1] + g[2] * a[2]

    for side, z in ((0, -1), (1, Z)):
        a, g, along = combine(z, 0, Y, lambda k: v2_far[k, side])
        c0[z + 1] = -a[0] * (g[0] * late[side, 1] + late[side, 0]) - late[side, 1] * along

    copies = []

    def send(n, source, target):
        copies.append(pltpu.make_async_copy(source, target, sems.at[n]))
        copies[-1].start()

    def coupling(z):
        a, g, along = combine(z, 0, Y, lambda k: v2[k, z + 1, 8 : 8 + Y])
        fl = [f[k, z] for k in range(3)]
        rest = g[0] * fl[0] + g[1] * fl[1] + g[2] * fl[2] + temporal[z]
        for k in range(3):
            adj[k, z] = a[k]
        send(z, adj.at[:, z], adj_out.at[:, z])
        c0[z + 1] = -a[0] * rest - fl[0] * along
        c1[z, 8 : 8 + Y] = -a[1] * rest - fl[1] * along
        c2[z] = -a[2] * rest - fl[2] * along
        out0[z] = along
        a, g, along = combine(z, Y, R, lambda k: v2[k, z + 1, 8 + Y : 8 + R])
        rows = [late_rows[k, z] for k in range(4)]
        rest = g[0] * rows[1] + g[1] * rows[2] + g[2] * rows[3] + rows[0]
        side = -a[1] * rest - rows[2] * along
        c1[z, 0:8] = side
        c1[z, 8 + Y : 16 + Y] = side

    def spread(z):
        left, right = lane_sides(c2[z])
        total = (c0[z + 2] - c0[z]) + (c1[z, 9 : 9 + Y] - c1[z, 7 : 7 + Y]) + (right - left)
        half = total * -0.25
        along = out0[z]
        out0[z] = half + along
        out1[z] = half - along
        send(Z + z, out0.at[z], out0_out.at[z])
        send(2 * Z + z, out1.at[z], out1_out.at[z])

    coupling(0)
    for z in range(1, Z):
        coupling(z)
        spread(z - 1)
    spread(Z - 1)
    for copy in copies:
        copy.wait()


def vmem(*dims):
    return pltpu.VMEM(dims, F32)


def pinned(array):
    return pltpu.with_memory_space_constraint(array, pltpu.VMEM)


def hbm(*arrays):
    return [pltpu.with_memory_space_constraint(array, pltpu.HBM) for array in arrays]


def shape(*dims):
    return jax.ShapeDtypeStruct(dims, F32)


def shards(image0, image1, flow, cotangent):
    nz, ny = lax.axis_size("gz"), lax.axis_size("gy")
    devices = nz * ny

    side, middle = pl.pallas_call(
        pack_rows,
        in_specs=[HB] * 4,
        out_specs=[VM] * 2,
        out_shape=[vmem(2, Z, 8, X)] * 2,
        scratch_shapes=[
            pltpu.VMEM((2, Z, 8, X), F32),
            pltpu.VMEM((2, Z, 8, X), F32),
            pltpu.VMEM((2, 3, Z, 8, X), F32),
            pltpu.VMEM((2, 3, Z, 8, X), F32),
            pltpu.SemaphoreType.DMA((2, 4)),
        ],
        compiler_params=params(8),
        name="pack_rows",
    )(*hbm(image0, image1, cotangent, flow))

    def swaps(count, start):
        pairs = [(i, i + 1) for i in range(start, count - 1, 2)]
        return pairs + [(j, i) for i, j in pairs]

    own_side = side
    middle = lax.ppermute(middle, "gy", swaps(ny, 1))
    side = lax.ppermute(side, "gy", swaps(ny, 0))

    fields = [vmem(1, Z + 4, PAD, X), vmem(3, Z + 4, PAD, X), vmem(3, Z + 2, PAD, X), vmem(3, Z + 2, R, X)]
    mean, b, temporal, flow = pl.pallas_call(
        load,
        in_specs=[HB] * 5,
        out_specs=[VM] * 4,
        out_shape=fields[:2] + [vmem(Z, Y, X), vmem(3, Z, Y, X)],
        scratch_shapes=[
            pltpu.VMEM((Z, Y, X), F32),
            pltpu.VMEM((Z, Y, X), F32),
            pltpu.SemaphoreType.DMA((4,)),
        ],
        compiler_params=params(12),
        name="load",
    )(*hbm(image0, image1, cotangent, flow), own_side)

    ring, late_rows, inner, outer = pl.pallas_call(
        pack_slabs,
        in_specs=[VM] * 4,
        out_specs=[VM] * 4,
        out_shape=[vmem(4, Z, 8, X)] * 2 + [vmem(4, 2 * Y + 8, X)] * 2,
        compiler_params=params(8),
        name="pack_slabs",
    )(mean, b, pinned(middle), pinned(side))
    outer = lax.ppermute(outer, "gz", swaps(nz, 1))
    inner = lax.ppermute(inner, "gz", swaps(nz, 0))

    *fields_own, own_sums, inner_far, outer_far = pl.pallas_call(
        krylov_own,
        in_specs=[VM] * 5,
        out_specs=[VM] * 7,
        out_shape=fields + [vmem(3, 8, X), vmem(5, Y, X), vmem(5, Y, X)],
        compiler_params=params(12),
        input_output_aliases={0: 0, 1: 1},
        name="krylov_own",
    )(mean, b, temporal, flow, ring)
    outer_far = lax.ppermute(outer_far, "gz", swaps(nz, 1))
    inner_far = lax.ppermute(inner_far, "gz", swaps(nz, 0))

    _, b, v1, grad, v2, near_sums = pl.pallas_call(
        krylov_near,
        in_specs=[VM] * 7,
        out_specs=[VM] * 6,
        out_shape=fields + [vmem(3, Z + 2, PAD, X), vmem(6, 8, X)],
        input_output_aliases={2 + n: n for n in range(4)},
        compiler_params=params(12),
        name="krylov_near",
    )(pinned(outer), pinned(inner), *fields_own, own_sums)

    v2_far, late, sums = pl.pallas_call(
        krylov_far,
        in_specs=[VM] * 6,
        out_specs=[VM] * 3,
        out_shape=[vmem(3, 2, Y, X), vmem(2, 2, Y, X), vmem(devices, 128)],
        compiler_params=params(12),
        name="krylov_far",
    )(pinned(outer_far), pinned(inner_far), v1, v2, grad, near_sums)

    sums = lax.all_to_all(sums.reshape(devices, 1, 128), ("gz", "gy"), 0, 0).reshape(devices, 128)

    return pl.pallas_call(
        finish,
        in_specs=[VM] * 10,
        out_specs=[HB] * 3,
        out_shape=[shape(3, Z, Y, X), shape(Z, Y, X), shape(Z, Y, X)],
        scratch_shapes=[
            pltpu.VMEM((3, Z, Y, X), F32),
            pltpu.VMEM((Z, Y, X), F32),
            pltpu.VMEM((Z, Y, X), F32),
            pltpu.VMEM((Z + 2, Y, X), F32),
            pltpu.VMEM((Z, Y + 16, X), F32),
            pltpu.VMEM((Z, Y, X), F32),
            pltpu.SemaphoreType.DMA((3 * Z,)),
        ],
        compiler_params=params(12),
        name="finish",
    )(sums, b, v1, v2, v2_far, grad, temporal, flow, late_rows, late)


def solution(mesh):
    return jax.shard_map(
        shards,
        mesh=mesh,
        in_specs=(
            P("gz", "gy", None),
            P("gz", "gy", None),
            P(None, "gz", "gy", None),
            P(None, "gz", "gy", None),
        ),
        out_specs=(P(None, "gz", "gy", None), P("gz", "gy", None), P("gz", "gy", None)),
        check_vma=False,
    )
```
